32 devices in a mesh: dp: 4 (over y, core), blk: 8 (over z, x).
Axes of the slice: x: 2, y: 2, z: 4, core: 2. Of those that a mesh axis runs over, the one named last changes fastest.
Arguments:
- q_raw: bfloat16 [4, 1024, 512], P('dp', 'blk'), may hold values from -8 to 8
- k_raw: bfloat16 [4, 1024, 128], P('dp', 'blk'), may hold values from -8 to 8
- values: bfloat16 [4, 1024, 128], P('dp', 'blk'), may hold values from -6 to 6
- out_grad: bfloat16 [4, 1024, 512], P('dp', 'blk'), may hold values from -60 to 60
- q_gain: float32 [128], replicated, may hold values from 0.5 to 5
- k_gain: float32 [128], replicated, may hold values from 0.5 to 5
- block_order: int32 [16], replicated, may hold values from 0 to 15, as said below
- seq_len: int32 [4], P('dp'), may hold values from 256 to 1024, as said below
Outputs:
- attended: bfloat16 [4, 1024, 512], P('dp', 'blk')
- q_grad: bfloat16 [4, 1024, 512], P('dp', 'blk')
- k_grad: bfloat16 [4, 1024, 128], P('dp', 'blk')
- v_grad: bfloat16 [4, 1024, 128], P('dp', 'blk')
- q_gain_grad: float32 [128], replicated
- k_gain_grad: float32 [128], replicated
The draws below stay inside these ranges and needn't reach their ends.
Inputs may be any that keep to these rules, and one draw needn't show every extreme that they name: `block_order`: each number from 0 to 15 appears exactly once. `seq_len`: some sequence is full and some holds exactly 256 valid tokens.
All inputs are finite; a program needn't handle non-finite values.
Results may differ from the reference program's by a relative error of at most 0.02.
The reference program's roundings to bfloat16 on the way count: a program that leaves them out, or rounds other values in their place, can miss the bound.
Values may be sent and summed in bfloat16 or wider, within the bound.
A program may use at most 64 MiB of HBM per device.

```python
import math
import jax
import jax.numpy as jnp
from jax import lax

HD = 128
QH = 4
SEQ = 1024
SEQS = 4
N_BLK = 8


def shared_keys(key):
    return jax.random.normal(jax.random.fold_in(key, 101), (SEQS, SEQ, HD), jnp.float32)


def log_uniform(key, dims, low_end, high_end):
    return jnp.exp(jax.random.uniform(key, dims, jnp.float32, math.log(low_end), math.log(high_end)))


def draw_k_raw(key, part):
    base_keys = shared_keys(key)
    return base_keys.astype(jnp.bfloat16)


def draw_q_raw(key, part):
    key = jax.random.fold_in(key, 2)
    fresh = jax.random.normal(key, (SEQS, SEQ, QH * HD), jnp.float32)
    return fresh.astype(jnp.bfloat16)


def draw_q_gain(key, part):
    key = jax.random.fold_in(key, 3)
    return log_uniform(key, (HD,), 0.5, 2.0)


def draw_k_gain(key, part):
    key = jax.random.fold_in(key, 4)
    return log_uniform(key, (HD,), 0.5, 2.0)


def draw_out_grad(key, part):
    key = jax.random.fold_in(key, 5)
    first_key, second_key = jax.random.split(key, 2)
    noise_rows = jax.random.normal(first_key, (SEQS, SEQ, QH * HD), jnp.float32)
    trend = 3.0 ** (jnp.arange(SEQ, dtype=jnp.float32) / SEQ)
    row_scale = log_uniform(second_key, (SEQS, SEQ, 1), 0.3, 3.0) * trend[None, :, None]
    return (noise_rows * row_scale).astype(jnp.bfloat16)


def draw_block_order(key, part):
    key = jax.random.fold_in(key, 6)
    return jax.random.permutation(key, 2 * N_BLK).astype(jnp.int32)


def draw_seq_len(key, part):
    key = jax.random.fold_in(key, 7)
    drawn = jax.random.randint(key, (SEQS,), SEQ // 4, SEQ + 1, jnp.int32)
    return drawn.at[0].set(SEQ).at[1].set(SEQ // 4)


def level_of(rng, extent, shards, least, largest):
    gain, own = 1.0, jax.random.fold_in(rng, 6)
    for axis_at, blocks in shards:
        heights = jnp.exp(jax.random.uniform(jax.random.fold_in(own, axis_at), (blocks,), jnp.float32, least / len(shards), largest / len(shards)))
        gain = gain * jnp.repeat(heights, extent[axis_at] // blocks).reshape([-1 if axis == axis_at else 1 for axis in range(len(extent))])
    return gain


def gaussian(rng, extent, width, limit, cuts=(), kind=jnp.bfloat16):
    gain = level_of(rng, extent, cuts, -0.22, 0.18) if cuts else 1.0
    values = jax.random.normal(rng, extent, jnp.float32) * width * gain
    return jnp.minimum(jnp.maximum(values, -limit), limit).astype(kind)


def setup_inputs(seed: int = 0) -> dict:
    key_list = jax.random.split(jax.random.key(seed), 9)
    q_raw = draw_q_raw(jax.random.fold_in(key_list[8], 71), 0)
    k_raw = draw_k_raw(jax.random.fold_in(key_list[8], 71), 0)
    values = gaussian(key_list[2], (SEQS, SEQ, HD), 1.0, 6.0, ((0, 4), (1, 8)))
    out_grad = draw_out_grad(jax.random.fold_in(key_list[8], 71), 0)
    q_gain = draw_q_gain(jax.random.fold_in(key_list[8], 71), 0)
    k_gain = draw_k_gain(jax.random.fold_in(key_list[8], 71), 0)
    block_order = draw_block_order(jax.random.fold_in(key_list[8], 71), 0)
    seq_len = draw_seq_len(jax.random.fold_in(key_list[8], 71), 0)
    return dict(q_raw=q_raw, k_raw=k_raw, values=values, out_grad=out_grad, q_gain=q_gain, k_gain=k_gain, block_order=block_order, seq_len=seq_len)


EPSILON = 1e-06

def rounded(array):
    return lax.optimization_barrier(array.astype(jnp.bfloat16)).astype(jnp.float32)

def norm_forward(raw_rows, gain_vec):
    inv_rms = lax.rsqrt(lax.optimization_barrier(jnp.mean(raw_rows * raw_rows, axis=-1, keepdims=True)) + EPSILON)
    return (raw_rows * inv_rms * gain_vec, inv_rms)

def norm_backward(raw_rows, inv_rms, gain_vec, grad_rows):
    scaled = gain_vec * grad_rows
    inner_mean = lax.optimization_barrier(jnp.mean(raw_rows * scaled, axis=-1, keepdims=True))
    d_raw = inv_rms * scaled - raw_rows * inv_rms ** 3 * inner_mean
    d_gain = lax.optimization_barrier(jnp.sum((grad_rows * raw_rows * inv_rms).reshape(-1, raw_rows.shape[-1]), axis=0))
    return (d_raw, d_gain)

def one_sequence(q_raw, k_raw, values, out_grad, seq_length, q_gain, k_gain, block_order):
    half_rows = SEQ // (2 * N_BLK)
    slot_ids = jnp.arange(SEQ, dtype=jnp.int32)
    positions = block_order[slot_ids // half_rows] * half_rows + slot_ids % half_rows
    key_live = positions < seq_length
    q_float = q_raw.astype(jnp.float32).reshape(SEQ, QH, HD)
    q_norm, q_inv = norm_forward(q_float, q_gain)
    q_hat = q_norm.astype(jnp.bfloat16)
    k_float = k_raw.astype(jnp.float32)
    k_norm, k_inv = norm_forward(k_float, k_gain)
    k_hat = k_norm.astype(jnp.bfloat16)
    key_float = k_hat.astype(jnp.float32)
    value_float = values.astype(jnp.float32)
    score_scale = HD ** (-0.5)
    query_block = min(SEQ, 512)
    query_blocks = SEQ // query_block

    def block_step(carried, block_index):
        dk_acc, dv_acc = carried
        row_start = block_index * query_block
        q_block = lax.dynamic_slice_in_dim(q_hat, row_start, query_block, 0).astype(jnp.float32)
        q_pos = lax.dynamic_slice_in_dim(positions, row_start, query_block, 0)
        q_live = lax.dynamic_slice_in_dim(key_live, row_start, query_block, 0)
        g_block = lax.dynamic_slice_in_dim(out_grad, row_start, query_block, 0)
        allowed = (positions[None, None, :] <= q_pos[:, None, None]) & key_live[None, None, :]
        scores = jnp.einsum('thd,kd->thk', q_block, key_float) * score_scale
        scores = jnp.where(allowed, scores, -jnp.inf)
        row_max = lax.optimization_barrier(jnp.max(scores, axis=-1))
        weights = jnp.exp(scores - row_max[..., None])
        row_sum = lax.optimization_barrier(jnp.sum(weights, axis=-1))
        mixed = jnp.einsum('thk,kd->thd', rounded(weights), value_float) / row_sum[..., None]
        out_block = jnp.where(q_live[:, None, None], mixed, 0.0).astype(jnp.bfloat16)
        log_total = row_max + jnp.log(row_sum)
        masked_grad = jnp.where(q_live[:, None], g_block, jnp.zeros_like(g_block)).reshape(query_block, QH, HD)
        grad_float = masked_grad.astype(jnp.float32)
        row_delta = lax.optimization_barrier(jnp.sum(grad_float * out_block.astype(jnp.float32), axis=-1))
        prob_rows = jnp.exp(scores - log_total[..., None])
        dv_acc = dv_acc + jnp.einsum('thk,thd->kd', rounded(prob_rows), grad_float)
        prob_grad = jnp.einsum('thd,kd->thk', grad_float, value_float)
        score_grad = rounded(prob_rows * (prob_grad - row_delta[..., None]) * score_scale)
        dq_block = jnp.einsum('thk,kd->thd', score_grad, key_float)
        dk_acc = dk_acc + jnp.einsum('thk,thd->kd', score_grad, q_block)
        return ((dk_acc, dv_acc), (out_block, dq_block))
    start_acc = (jnp.zeros((SEQ, HD), jnp.float32), jnp.zeros((SEQ, HD), jnp.float32))
    carried, stacked = lax.scan(block_step, start_acc, jnp.arange(query_blocks, dtype=jnp.int32))
    dk_hat, dv_acc = carried
    out_blocks, dq_blocks = stacked
    dq_hat = dq_blocks.reshape(SEQ, QH, HD)
    q_grad, q_gain_part = norm_backward(q_float, q_inv, q_gain, dq_hat)
    k_grad, k_gain_part = norm_backward(k_float, k_inv, k_gain, dk_hat)
    return (out_blocks.reshape(SEQ, QH * HD), q_grad.astype(jnp.bfloat16).reshape(SEQ, QH * HD), k_grad.astype(jnp.bfloat16), dv_acc.astype(jnp.bfloat16), q_gain_part, k_gain_part)

def reference(q_raw, k_raw, values, out_grad, q_gain, k_gain, block_order, seq_len):

    def per_sequence(items):
        return one_sequence(items[0], items[1], items[2], items[3], items[4], q_gain, k_gain, block_order)
    results = lax.map(per_sequence, (q_raw, k_raw, values, out_grad, seq_len))
    attended, q_grad, k_grad, v_grad, q_gain_parts, k_gain_parts = results
    return (attended, q_grad, k_grad, v_grad, lax.optimization_barrier(jnp.sum(q_gain_parts, axis=0)), lax.optimization_barrier(jnp.sum(k_gain_parts, axis=0)))
```

```python
import functools

import jax
import jax.numpy as jnp
from jax import lax
from jax.experimental import pallas as pl
from jax.experimental.pallas import tpu as pltpu
from jax.sharding import PartitionSpec as P

EPSILON = 1e-06
MASKED = -1e30
FAR = 1 << 30
LOG2E = 1.4426950408889634
F32 = jnp.float32
BF16 = jnp.bfloat16


def loop(low, high, body, carry):
    if high - low <= 8:
        for i in range(low, high):
            carry = body(i, carry)
        return carry
    return lax.fori_loop(low, high, body, carry)


def dot_nt(a, b):
    return lax.dot_general(a, b, (((1,), (1,)), ((), ())), preferred_element_type=F32)


def dot_nn(a, b):
    return lax.dot_general(a, b, (((1,), (0,)), ((), ())), preferred_element_type=F32)


def dot_tn(a, b):
    return lax.dot_general(a, b, (((0,), (0,)), ((), ())), preferred_element_type=F32)


def kernel(
    n, groups, order_ref, len_ref, q_ref, k_ref, v_ref, go_ref, qg_ref, kg_ref,
    att_ref, qgrad_ref, kgrad_ref, vgrad_ref, qgain_ref, kgain_ref,
    kv, score, pgrad, dsend, drecv, gain1, gain2, q_hats, g_rows,
    kv_send, kv_recv, d_send, d_recv, g1_send, g1_recv, g2_send, g2_recv,
):
    rows, hd = k_ref.shape
    heads = q_ref.shape[1] // hd
    half = rows // 2
    me = lax.axis_index("blk")
    group = lax.axis_index("dp")
    scale = hd ** (-0.5)

    barrier = pltpu.get_barrier_semaphore()

    def greet(i, _):
        pl.semaphore_signal(barrier, inc=1, device_id={"blk": lax.rem(me + i, n)}, device_id_type=pl.DeviceIdType.MESH)
        return _

    def greet_group(i, _):
        pl.semaphore_signal(barrier, inc=1, device_id={"dp": lax.rem(group + i, groups)}, device_id_type=pl.DeviceIdType.MESH)
        return _

    loop(1, n, greet, 0)
    loop(1, groups, greet_group, 0)

    def kv_copy(i):
        return pltpu.make_async_remote_copy(
            src_ref=kv.at[0], dst_ref=kv.at[i], send_sem=kv_send.at[i], recv_sem=kv_recv.at[i],
            device_id={"blk": lax.rem(me + i, n)}, device_id_type=pl.DeviceIdType.MESH)

    def d_copy(i):
        return pltpu.make_async_remote_copy(
            src_ref=dsend.at[i], dst_ref=drecv.at[i], send_sem=d_send.at[i], recv_sem=d_recv.at[i],
            device_id={"blk": lax.rem(me - i + n, n)}, device_id_type=pl.DeviceIdType.MESH)

    def g1_copy(i, slot):
        return pltpu.make_async_remote_copy(
            src_ref=gain1.at[slot], dst_ref=gain1.at[slot], send_sem=g1_send.at[i], recv_sem=g1_recv.at[i],
            device_id={"blk": lax.rem(me + i, n)}, device_id_type=pl.DeviceIdType.MESH)

    def g2_copy(i, slot):
        return pltpu.make_async_remote_copy(
            src_ref=gain2.at[slot], dst_ref=gain2.at[slot], send_sem=g2_send.at[i], recv_sem=g2_recv.at[i],
            device_id={"dp": lax.rem(group + i, groups)}, device_id_type=pl.DeviceIdType.MESH)

    k_gain = kg_ref[...]
    q_gain = qg_ref[...]
    k_float = k_ref[...].astype(F32)
    k_inv = lax.rsqrt(jnp.mean(k_float * k_float, axis=-1, keepdims=True) + EPSILON)
    kv[0, :, :hd] = (k_float * k_inv * k_gain).astype(BF16)
    kv[0, :, hd:] = v_ref[...]

    pl.semaphore_wait(barrier, n - 1 + groups - 1)

    def start_kv(i, _):
        kv_copy(i).start()
        return _

    loop(1, n, start_kv, 0)

    seq_length = len_ref[0]

    def positions(owner, axis, shape):
        ids = lax.broadcasted_iota(jnp.int32, shape, axis)
        first = order_ref[2 * owner] * half
        second = order_ref[2 * owner + 1] * half - half
        return ids + jnp.where(ids < half, first, second)

    q_pos = jnp.concatenate([positions(me, 1, (1, rows))] * heads, axis=1)
    live_lane = q_pos < seq_length
    live_rows = positions(me, 0, (rows, hd)) < seq_length
    q_invs = []
    g_cols = []
    for h in range(heads):
        cut = slice(h * hd, (h + 1) * hd)
        q_float = q_ref[:, cut].astype(F32)
        q_inv = lax.rsqrt(jnp.mean(q_float * q_float, axis=-1, keepdims=True) + EPSILON)
        q_invs.append(q_inv)
        q_hats[h * rows:(h + 1) * rows, :] = (q_float * q_inv * q_gain).astype(BF16)
        g_float = jnp.where(live_rows, go_ref[:, cut].astype(F32), 0.0)
        g_rows[h * rows:(h + 1) * rows, :] = g_float.astype(BF16)
        g_cols.append(jnp.transpose(g_float))
    g_cols = jnp.concatenate(g_cols, axis=1)

    def first_pass(i, top):
        k_pos = positions(lax.rem(me - i + n, n), 0, (rows, heads * rows))
        k_pos = jnp.where(k_pos < seq_length, k_pos, FAR)
        s = dot_nt(kv[i, :, :hd], q_hats[...]) * (scale * LOG2E)
        s = jnp.where(k_pos <= q_pos, s, MASKED)
        score[i] = s
        pgrad[i] = dot_nt(kv[i, :, hd:], g_rows[...])
        return jnp.maximum(top, jnp.max(s, axis=0, keepdims=True))

    def first_pass_remote(i, top):
        kv_copy(i).wait_recv()
        return first_pass(i, top)

    top = first_pass(0, jnp.full((1, heads * rows), MASKED, F32))
    top = loop(1, n, first_pass_remote, top)

    def second_pass(i, carry):
        total, mixed = carry
        w = jnp.exp2(score[i] - top)
        score[i] = w
        total = total + jnp.sum(w, axis=0, keepdims=True)
        mixed = mixed + dot_tn(kv[i, :, hd:], w.astype(BF16))
        return total, mixed

    total, mixed = loop(
        0, n, second_pass,
        (jnp.zeros((1, heads * rows), F32), jnp.zeros((hd, heads * rows), F32)))
    inverse = 1.0 / total
    attended = jnp.where(live_lane, mixed * inverse, 0.0).astype(BF16).astype(F32)
    delta = jnp.sum(attended * g_cols, axis=0, keepdims=True)

    def third_pass(i, dq):
        p = score[i] * inverse
        ds = (p * (pgrad[i] - delta) * scale).astype(BF16)
        dk = dot_nn(ds, q_hats[...])
        dv = dot_nn(p.astype(BF16), g_rows[...])
        dq = dq + dot_tn(kv[i, :, :hd], ds)
        return dq, dk, dv

    def third_pass_remote(i, dq):
        dq, dk, dv = third_pass(i, dq)
        dsend[i, :, :hd] = dk.astype(BF16)
        dsend[i, :, hd:] = dv.astype(BF16)
        d_copy(i).start()
        return dq

    dq = loop(1, n, third_pass_remote, jnp.zeros((hd, heads * rows), F32))
    dq, dk, dv = third_pass(0, dq)

    part_q = jnp.zeros((1, hd), F32)
    part_k = jnp.zeros((1, hd), F32)
    dq_rows = []
    for h in range(heads):
        cut = slice(h * hd, (h + 1) * hd)
        dq_h = jnp.transpose(dq[:, h * rows:(h + 1) * rows])
        dq_rows.append(dq_h)
        q_float = q_ref[:, cut].astype(F32)
        part_q = part_q + jnp.sum(dq_h * q_float * q_invs[h], axis=0, keepdims=True)
        q_hat = q_hats[h * rows:(h + 1) * rows, :].astype(F32)
        part_k = part_k + jnp.sum(dq_h * q_hat, axis=0, keepdims=True)
    gain1[me, 0:1, :] = part_q
    gain1[me, 1:2, :] = part_k / k_gain

    def start_g1(i, _):
        g1_copy(i, me).start()
        return _

    loop(1, n, start_g1, 0)

    for h in range(heads):
        cut = slice(h * hd, (h + 1) * hd)
        q_float = q_ref[:, cut].astype(F32)
        q_inv = q_invs[h]
        scaled = q_gain * dq_rows[h]
        inner = jnp.mean(q_float * scaled, axis=-1, keepdims=True)
        qgrad_ref[:, cut] = (q_inv * scaled - q_float * (q_inv * q_inv * q_inv * inner)).astype(BF16)
        att_ref[:, cut] = jnp.transpose(attended[:, h * rows:(h + 1) * rows]).astype(BF16)

    def wait_g1(i, _):
        g1_copy(i, lax.rem(me - i + n, n)).wait_recv()
        return _

    loop(1, n, wait_g1, 0)
    gain2[group] = loop(1, n, lambda i, acc: acc + gain1[i], gain1[0])

    def start_g2(i, _):
        g2_copy(i, group).start()
        return _

    loop(1, groups, start_g2, 0)

    def gather(i, carry):
        dk, dv = carry
        d_copy(i).wait_recv()
        return dk + drecv[i, :, :hd].astype(F32), dv + drecv[i, :, hd:].astype(F32)

    dk, dv = loop(1, n, gather, (dk, dv))
    vgrad_ref[...] = dv.astype(BF16)
    scaled = k_gain * dk
    inner = jnp.mean(k_float * scaled, axis=-1, keepdims=True)
    kgrad_ref[...] = (k_inv * scaled - k_float * (k_inv * k_inv * k_inv * inner)).astype(BF16)

    def wait_g2(i, _):
        g2_copy(i, lax.rem(group - i + groups, groups)).wait_recv()
        return _

    loop(1, groups, wait_g2, 0)
    gains = loop(1, groups, lambda i, acc: acc + gain2[i], gain2[0])
    qgain_ref[...] = gains[0:1, :]
    kgain_ref[...] = gains[1:2, :]

    def drain(i, _):
        kv_copy(i).wait_send()
        d_copy(i).wait_send()
        g1_copy(i, me).wait_send()
        return _

    loop(1, n, drain, 0)

    def drain_group(i, _):
        g2_copy(i, group).wait_send()
        return _

    loop(1, groups, drain_group, 0)


def per_device(n, groups, q_raw, k_raw, values, out_grad, q_gain, k_gain, block_order, seq_len):
    rows, wide = q_raw.shape[1:]
    hd = k_raw.shape[2]
    lanes = (wide // hd) * rows
    vmem = pl.BlockSpec(memory_space=pltpu.VMEM)
    smem = pl.BlockSpec(memory_space=pltpu.SMEM)
    dma = pltpu.SemaphoreType.DMA
    out = pl.pallas_call(
        functools.partial(kernel, n, groups),
        out_shape=[
            jax.ShapeDtypeStruct((rows, wide), BF16),
            jax.ShapeDtypeStruct((rows, wide), BF16),
            jax.ShapeDtypeStruct((rows, hd), BF16),
            jax.ShapeDtypeStruct((rows, hd), BF16),
            jax.ShapeDtypeStruct((1, hd), F32),
            jax.ShapeDtypeStruct((1, hd), F32),
        ],
        in_specs=[smem, smem] + [vmem] * 6,
        out_specs=[vmem] * 6,
        scratch_shapes=[
            pltpu.VMEM((n, rows, 2 * hd), BF16),
            pltpu.VMEM((n, rows, lanes), F32),
            pltpu.VMEM((n, rows, lanes), F32),
            pltpu.VMEM((n, rows, 2 * hd), BF16),
            pltpu.VMEM((n, rows, 2 * hd), BF16),
            pltpu.VMEM((n, 2, hd), F32),
            pltpu.VMEM((groups, 2, hd), F32),
            pltpu.VMEM((lanes, hd), BF16),
            pltpu.VMEM((lanes, hd), BF16),
            dma((n,)), dma((n,)), dma((n,)), dma((n,)),
            dma((n,)), dma((n,)), dma((groups,)), dma((groups,)),
        ],
        compiler_params=pltpu.CompilerParams(
            collective_id=0, has_side_effects=True,
            vmem_limit_bytes=(16 + n) * 2**20),
    )(
        block_order, seq_len, q_raw[0], k_raw[0], values[0], out_grad[0],
        q_gain[None], k_gain[None],
    )
    attended, q_grad, k_grad, v_grad, q_gain_grad, k_gain_grad = out
    return (attended[None], q_grad[None], k_grad[None], v_grad[None], q_gain_grad[0], k_gain_grad[0])


def solution(mesh):
    tokens = P("dp", "blk", None)
    in_specs = (tokens, tokens, tokens, tokens, P(), P(), P(), P("dp"))
    out_specs = (tokens, tokens, tokens, tokens, P(), P())
    return jax.shard_map(
        functools.partial(per_device, mesh.shape["blk"], mesh.shape["dp"]),
        mesh=mesh, in_specs=in_specs, out_specs=out_specs, check_vma=False)
```

```python
import functools

import jax
import jax.numpy as jnp
from jax import lax
from jax.experimental import pallas as pl
from jax.experimental.pallas import tpu as pltpu
from jax.sharding import PartitionSpec as P

EPSILON = 1e-06
MASKED = -1e30
FAR = 1 << 30
LOG2E = 1.4426950408889634
F32 = jnp.float32
BF16 = jnp.bfloat16


def loop(low, high, body, carry):
    if high - low <= 8:
        for i in range(low, high):
            carry = body(i, carry)
        return carry
    return lax.fori_loop(low, high, body, carry)


def dot_nt(a, b):
    return lax.dot_general(a, b, (((1,), (1,)), ((), ())), preferred_element_type=F32)


def dot_nn(a, b):
    return lax.dot_general(a, b, (((1,), (0,)), ((), ())), preferred_element_type=F32)


def dot_tn(a, b):
    return lax.dot_general(a, b, (((0,), (0,)), ((), ())), preferred_element_type=F32)


def kernel(
    n, groups, order_ref, len_ref, q_hbm, k_hbm, v_hbm, go_hbm, qg_hbm, kg_hbm,
    att_hbm, qgrad_hbm, kgrad_hbm, vgrad_hbm, qgain_hbm, kgain_hbm,
    q_ref, k_ref, go_ref, qg_ref, kg_ref, in_sem,
    att_ref, qgrad_ref, kgrad_ref, vgrad_ref, qgain_ref, kgain_ref, out_sem,
    kv, score, pgrad, xsend, xrecv, zsend, zrecv, gain1, gain2, q_hats, g_rows,
    kv_send, kv_recv, x_send, x_recv, z_send, z_recv, g1_send, g1_recv, g2_send, g2_recv,
):
    rows, hd = k_ref.shape
    heads = q_ref.shape[1] // hd
    half = rows // 2
    me = lax.axis_index("blk")
    group = lax.axis_index("dp")
    scale = hd ** (-0.5)
    lines = n // 2
    line, side = me // 2, lax.rem(me, 2)
    partner = 2 * line + 1 - side

    def owner_of(slot):
        other = lax.rem(side + slot % 2, 2)
        return 2 * lax.rem(line - slot // 2 + lines, lines) + other

    loads = [
        pltpu.make_async_copy(src, dst, in_sem.at[i]) for i, (src, dst) in enumerate([
            (k_hbm, k_ref), (kg_hbm, kg_ref), (v_hbm, kv.at[0, :, pl.ds(hd, hd)]),
            (q_hbm, q_ref), (qg_hbm, qg_ref), (go_hbm, go_ref)])]
    for load in loads:
        load.start()

    stores = [
        pltpu.make_async_copy(src, dst, out_sem.at[i]) for i, (src, dst) in enumerate([
            (att_ref, att_hbm), (qgrad_ref, qgrad_hbm), (vgrad_ref, vgrad_hbm),
            (kgrad_ref, kgrad_hbm), (qgain_ref, qgain_hbm), (kgain_ref, kgain_hbm)])]

    barrier = pltpu.get_barrier_semaphore()

    def greet(i, _):
        pl.semaphore_signal(barrier, inc=1, device_id={"blk": lax.rem(me + i, n)}, device_id_type=pl.DeviceIdType.MESH)
        return _

    def greet_group(i, _):
        pl.semaphore_signal(barrier, inc=1, device_id={"dp": lax.rem(group + i, groups)}, device_id_type=pl.DeviceIdType.MESH)
        return _

    loop(1, n, greet, 0)
    loop(1, groups, greet_group, 0)

    def push(src, dst, send, recv, i, device):
        return pltpu.make_async_remote_copy(
            src_ref=src, dst_ref=dst, send_sem=send.at[i], recv_sem=recv.at[i],
            device_id={"blk": device}, device_id_type=pl.DeviceIdType.MESH)

    def kv_line(j):
        device = 2 * lax.rem(line + j, lines) + side
        return push(kv.at[0], kv.at[2 * j], kv_send, kv_recv, 2 * j, device)

    def kv_side(j):
        return push(kv.at[2 * j], kv.at[2 * j + 1], kv_send, kv_recv, 2 * j + 1, partner)

    def d_side(j):
        return push(xsend.at[j], xrecv.at[j], x_send, x_recv, j, partner)

    def d_line(j):
        device = 2 * lax.rem(line - j + lines, lines) + side
        return push(zsend.at[j], zrecv.at[j], z_send, z_recv, j, device)

    def g1_copy(i, slot):
        return pltpu.make_async_remote_copy(
            src_ref=gain1.at[slot], dst_ref=gain1.at[slot], send_sem=g1_send.at[i], recv_sem=g1_recv.at[i],
            device_id={"blk": lax.rem(me + i, n)}, device_id_type=pl.DeviceIdType.MESH)

    def g2_copy(i, slot):
        return pltpu.make_async_remote_copy(
            src_ref=gain2.at[slot], dst_ref=gain2.at[slot], send_sem=g2_send.at[i], recv_sem=g2_recv.at[i],
            device_id={"dp": lax.rem(group + i, groups)}, device_id_type=pl.DeviceIdType.MESH)

    for load in loads[:3]:
        load.wait()
    k_gain = kg_ref[...]
    k_float = k_ref[...].astype(F32)
    k_inv = lax.rsqrt(jnp.mean(k_float * k_float, axis=-1, keepdims=True) + EPSILON)
    kv[0, :, :hd] = (k_float * k_inv * k_gain).astype(BF16)

    pl.semaphore_wait(barrier, n - 1 + groups - 1)

    kv_side(0).start()

    def start_kv(j, _):
        kv_line(j).start()
        return _

    loop(1, lines, start_kv, 0)
    for load in loads[3:]:
        load.wait()
    q_gain = qg_ref[...]

    seq_length = len_ref[0]

    def positions(owner, axis, shape):
        ids = lax.broadcasted_iota(jnp.int32, shape, axis)
        first = order_ref[2 * owner] * half
        second = order_ref[2 * owner + 1] * half - half
        return ids + jnp.where(ids < half, first, second)

    q_pos = jnp.concatenate([positions(me, 1, (1, rows))] * heads, axis=1)
    live_lane = q_pos < seq_length
    live_rows = positions(me, 0, (rows, hd)) < seq_length
    q_invs = []
    g_cols = []
    for h in range(heads):
        cut = slice(h * hd, (h + 1) * hd)
        q_float = q_ref[:, cut].astype(F32)
        q_inv = lax.rsqrt(jnp.mean(q_float * q_float, axis=-1, keepdims=True) + EPSILON)
        q_invs.append(q_inv)
        q_hats[h * rows:(h + 1) * rows, :] = (q_float * q_inv * q_gain).astype(BF16)
        g_float = jnp.where(live_rows, go_ref[:, cut].astype(F32), 0.0)
        g_rows[h * rows:(h + 1) * rows, :] = g_float.astype(BF16)
        g_cols.append(jnp.transpose(g_float))
    g_cols = jnp.concatenate(g_cols, axis=1)

    def first_pass(i, top):
        k_pos = positions(owner_of(i), 0, (rows, heads * rows))
        k_pos = jnp.where(k_pos < seq_length, k_pos, FAR)
        s = dot_nt(kv[i, :, :hd], q_hats[...]) * (scale * LOG2E)
        s = jnp.where(k_pos <= q_pos, s, MASKED)
        score[i] = s
        pgrad[i] = dot_nt(kv[i, :, hd:], g_rows[...])
        return jnp.maximum(top, jnp.max(s, axis=0, keepdims=True))

    def first_pass_remote(j, top):
        kv_line(j).wait_recv()
        kv_side(j).start()
        top = first_pass(2 * j, top)
        kv_side(j - 1).wait_recv()
        return first_pass(2 * j - 1, top)

    top = first_pass(0, jnp.full((1, heads * rows), MASKED, F32))
    top = loop(1, lines, first_pass_remote, top)
    kv_side(lines - 1).wait_recv()
    top = first_pass(n - 1, top)

    def second_pass(i, carry):
        total, mixed = carry
        w = jnp.exp2(score[i] - top)
        score[i] = w
        total = total + jnp.sum(w, axis=0, keepdims=True)
        mixed = mixed + dot_tn(kv[i, :, hd:], w.astype(BF16))
        return total, mixed

    total, mixed = loop(
        0, n, second_pass,
        (jnp.zeros((1, heads * rows), F32), jnp.zeros((hd, heads * rows), F32)))
    inverse = 1.0 / total
    attended = jnp.where(live_lane, mixed * inverse, 0.0).astype(BF16).astype(F32)
    delta = jnp.sum(attended * g_cols, axis=0, keepdims=True)

    def third_pass(i, dq):
        p = score[i] * inverse
        ds = (p * (pgrad[i] - delta) * scale).astype(BF16)
        dk = dot_nn(ds, q_hats[...])
        dv = dot_nn(p.astype(BF16), g_rows[...])
        dq = dq + dot_tn(kv[i, :, :hd], ds)
        return dq, dk, dv

    def other_side(step, dq):
        j = (step + 1) % lines
        dq, dk, dv = third_pass(2 * j + 1, dq)
        xsend[j, :, :hd] = dk.astype(BF16)
        xsend[j, :, hd:] = dv.astype(BF16)
        d_side(j).start()
        return dq

    def own_side(j, dq):
        dq, dk, dv = third_pass(2 * j, dq)
        d_side(j).wait_recv()
        zsend[j, :, :hd] = (dk + xrecv[j, :, :hd].astype(F32)).astype(BF16)
        zsend[j, :, hd:] = (dv + xrecv[j, :, hd:].astype(F32)).astype(BF16)
        d_line(j).start()
        return dq

    dq = loop(0, lines, other_side, jnp.zeros((hd, heads * rows), F32))
    dq = loop(1, lines, own_side, dq)
    dq, dk, dv = third_pass(0, dq)

    part_q = jnp.zeros((1, hd), F32)
    part_k = jnp.zeros((1, hd), F32)
    dq_rows = []
    for h in range(heads):
        cut = slice(h * hd, (h + 1) * hd)
        dq_h = jnp.transpose(dq[:, h * rows:(h + 1) * rows])
        dq_rows.append(dq_h)
        q_float = q_ref[:, cut].astype(F32)
        part_q = part_q + jnp.sum(dq_h * q_float * q_invs[h], axis=0, keepdims=True)
        q_hat = q_hats[h * rows:(h + 1) * rows, :].astype(F32)
        part_k = part_k + jnp.sum(dq_h * q_hat, axis=0, keepdims=True)
    gain1[me, 0:1, :] = part_q
    gain1[me, 1:2, :] = part_k / k_gain

    def start_g1(i, _):
        g1_copy(i, me).start()
        return _

    loop(1, n, start_g1, 0)

    for h in range(heads):
        cut = slice(h * hd, (h + 1) * hd)
        q_float = q_ref[:, cut].astype(F32)
        q_inv = q_invs[h]
        scaled = q_gain * dq_rows[h]
        inner = jnp.mean(q_float * scaled, axis=-1, keepdims=True)
        qgrad_ref[:, cut] = (q_inv * scaled - q_float * (q_inv * q_inv * q_inv * inner)).astype(BF16)
        att_ref[:, cut] = jnp.transpose(attended[:, h * rows:(h + 1) * rows]).astype(BF16)

    stores[0].start()
    stores[1].start()

    def wait_g1(i, _):
        g1_copy(i, lax.rem(me - i + n, n)).wait_recv()
        return _

    loop(1, n, wait_g1, 0)
    gain2[group] = loop(1, n, lambda i, acc: acc + gain1[i], gain1[0])

    def start_g2(i, _):
        g2_copy(i, group).start()
        return _

    loop(1, groups, start_g2, 0)

    d_side(0).wait_recv()
    dk = dk + xrecv[0, :, :hd].astype(F32)
    dv = dv + xrecv[0, :, hd:].astype(F32)

    def gather(j, carry):
        dk, dv = carry
        d_line(j).wait_recv()
        return dk + zrecv[j, :, :hd].astype(F32), dv + zrecv[j, :, hd:].astype(F32)

    dk, dv = loop(1, lines, gather, (dk, dv))
    vgrad_ref[...] = dv.astype(BF16)
    stores[2].start()
    scaled = k_gain * dk
    inner = jnp.mean(k_float * scaled, axis=-1, keepdims=True)
    kgrad_ref[...] = (k_inv * scaled - k_float * (k_inv * k_inv * k_inv * inner)).astype(BF16)

    stores[3].start()

    def wait_g2(i, _):
        g2_copy(i, lax.rem(group - i + groups, groups)).wait_recv()
        return _

    loop(1, groups, wait_g2, 0)
    gains = loop(1, groups, lambda i, acc: acc + gain2[i], gain2[0])
    qgain_ref[...] = gains[0:1, :]
    kgain_ref[...] = gains[1:2, :]
    stores[4].start()
    stores[5].start()

    def drain(i, _):
        g1_copy(i, me).wait_send()
        return _

    loop(1, n, drain, 0)

    def drain_side(j, _):
        kv_side(j).wait_send()
        d_side(j).wait_send()
        return _

    def drain_line(j, _):
        kv_line(j).wait_send()
        d_line(j).wait_send()
        return _

    loop(0, lines, drain_side, 0)
    loop(1, lines, drain_line, 0)

    def drain_group(i, _):
        g2_copy(i, group).wait_send()
        return _

    loop(1, groups, drain_group, 0)
    for store in stores:
        store.wait()


def store_kernel(*refs):
    count = len(refs) // 2
    sems = refs[2 * count]
    copies = [pltpu.make_async_copy(refs[i], refs[count + i], sems.at[i]) for i in range(count)]
    for copy in copies:
        copy.start()
    for copy in copies:
        copy.wait()


def per_device(n, groups, q_raw, k_raw, values, out_grad, q_gain, k_gain, block_order, seq_len):
    rows, wide = q_raw.shape[1:]
    hd = k_raw.shape[2]
    lanes = (wide // hd) * rows
    hbm = pl.BlockSpec(memory_space=pltpu.HBM)
    smem = pl.BlockSpec(memory_space=pltpu.SMEM)
    dma = pltpu.SemaphoreType.DMA
    out = pl.pallas_call(
        functools.partial(kernel, n, groups),
        out_shape=[
            jax.ShapeDtypeStruct((rows, wide), BF16),
            jax.ShapeDtypeStruct((rows, wide), BF16),
            jax.ShapeDtypeStruct((rows, hd), BF16),
            jax.ShapeDtypeStruct((rows, hd), BF16),
            jax.ShapeDtypeStruct((1, hd), F32),
            jax.ShapeDtypeStruct((1, hd), F32),
        ],
        in_specs=[smem, smem] + [hbm] * 6,
        out_specs=[hbm] * 6,
        scratch_shapes=[
            pltpu.VMEM((rows, wide), BF16),
            pltpu.VMEM((rows, hd), BF16),
            pltpu.VMEM((rows, wide), BF16),
            pltpu.VMEM((1, hd), F32),
            pltpu.VMEM((1, hd), F32),
            dma((6,)),
            pltpu.VMEM((rows, wide), BF16),
            pltpu.VMEM((rows, wide), BF16),
            pltpu.VMEM((rows, hd), BF16),
            pltpu.VMEM((rows, hd), BF16),
            pltpu.VMEM((1, hd), F32),
            pltpu.VMEM((1, hd), F32),
            dma((6,)),
            pltpu.VMEM((n, rows, 2 * hd), BF16),
            pltpu.VMEM((n, rows, lanes), F32),
            pltpu.VMEM((n, rows, lanes), F32),
            pltpu.VMEM((n // 2, rows, 2 * hd), BF16),
            pltpu.VMEM((n // 2, rows, 2 * hd), BF16),
            pltpu.VMEM((n // 2, rows, 2 * hd), BF16),
            pltpu.VMEM((n // 2, rows, 2 * hd), BF16),
            pltpu.VMEM((n, 2, hd), F32),
            pltpu.VMEM((groups, 2, hd), F32),
            pltpu.VMEM((lanes, hd), BF16),
            pltpu.VMEM((lanes, hd), BF16),
            dma((n,)), dma((n,)),
            dma((n // 2,)), dma((n // 2,)), dma((n // 2,)), dma((n // 2,)),
            dma((n,)), dma((n,)), dma((groups,)), dma((groups,)),
        ],
        compiler_params=pltpu.CompilerParams(
            collective_id=0, has_side_effects=True,
            vmem_limit_bytes=60 * 2**20),
    )(
        block_order, seq_len, q_raw[0], k_raw[0], values[0], out_grad[0],
        q_gain[None], k_gain[None],
    )
    out = pl.pallas_call(
        store_kernel,
        out_shape=[jax.ShapeDtypeStruct(o.shape, o.dtype) for o in out],
        in_specs=[hbm] * len(out),
        out_specs=[hbm] * len(out),
        scratch_shapes=[dma((len(out),))],
        compiler_params=pltpu.CompilerParams(vmem_limit_bytes=60 * 2**20),
    )(*out)
    attended, q_grad, k_grad, v_grad, q_gain_grad, k_gain_grad = out
    return (attended[None], q_grad[None], k_grad[None], v_grad[None], q_gain_grad[0], k_gain_grad[0])


def solution(mesh):
    tokens = P("dp", "blk", None)
    in_specs = (tokens, tokens, tokens, tokens, P(), P(), P(), P("dp"))
    out_specs = (tokens, tokens, tokens, tokens, P(), P())
    return jax.shard_map(
        functools.partial(per_device, mesh.shape["blk"], mesh.shape["dp"]),
        mesh=mesh, in_specs=in_specs, out_specs=out_specs, check_vma=False)
```

```python
import functools

import jax
import jax.numpy as jnp
from jax import lax
from jax.experimental import pallas as pl
from jax.experimental.pallas import tpu as pltpu
from jax.sharding import PartitionSpec as P

EPSILON = 1e-06
MASKED = -1e30
FAR = 1 << 30
LOG2E = 1.4426950408889634
F32 = jnp.float32
BF16 = jnp.bfloat16


def loop(low, high, body, carry):
    if high - low <= 8:
        for i in range(low, high):
            carry = body(i, carry)
        return carry
    return lax.fori_loop(low, high, body, carry)


def dot_nt(a, b):
    return lax.dot_general(a, b, (((1,), (1,)), ((), ())), preferred_element_type=F32)


def dot_nn(a, b):
    return lax.dot_general(a, b, (((1,), (0,)), ((), ())), preferred_element_type=F32)


def dot_tn(a, b):
    return lax.dot_general(a, b, (((0,), (0,)), ((), ())), preferred_element_type=F32)


def kernel(
    n, groups, order_ref, len_ref, q_hbm, k_hbm, v_hbm, go_hbm, qg_hbm, kg_hbm,
    att_hbm, qgrad_hbm, kgrad_hbm, vgrad_hbm, qgain_hbm, kgain_hbm,
    q_ref, k_ref, go_ref, qg_ref, kg_ref, in_sem,
    att_ref, qgrad_ref, kgrad_ref, vgrad_ref, qgain_ref, kgain_ref, out_sem,
    kv, score, pgrad, xsend, xrecv, zsend, zrecv, gain1, gain2, q_hats, g_rows,
    kv_send, kv_recv, x_send, x_recv, z_send, z_recv, g1_send, g1_recv, g2_send, g2_recv,
):
    rows, hd = k_ref.shape
    heads = q_ref.shape[1] // hd
    half = rows // 2
    me = lax.axis_index("blk")
    group = lax.axis_index("dp")
    scale = hd ** (-0.5)
    lines = n // 2
    line, side = me // 2, lax.rem(me, 2)
    partner = 2 * line + 1 - side

    def owner_of(slot):
        other = lax.rem(side + slot % 2, 2)
        return 2 * lax.rem(line - slot // 2 + lines, lines) + other

    loads = [
        pltpu.make_async_copy(src, dst, in_sem.at[i]) for i, (src, dst) in enumerate([
            (k_hbm, k_ref), (kg_hbm, kg_ref), (v_hbm, kv.at[0, :, pl.ds(hd, hd)]),
            (q_hbm, q_ref), (qg_hbm, qg_ref), (go_hbm, go_ref)])]
    for load in loads:
        load.start()

    stores = [
        pltpu.make_async_copy(src, dst, out_sem.at[i]) for i, (src, dst) in enumerate([
            (att_ref, att_hbm), (qgrad_ref, qgrad_hbm), (vgrad_ref, vgrad_hbm),
            (kgrad_ref, kgrad_hbm), (qgain_ref, qgain_hbm), (kgain_ref, kgain_hbm)])]

    barrier = pltpu.get_barrier_semaphore()

    def greet(i, _):
        pl.semaphore_signal(barrier, inc=1, device_id={"blk": lax.rem(me + i, n)}, device_id_type=pl.DeviceIdType.MESH)
        return _

    def greet_group(i, _):
        pl.semaphore_signal(barrier, inc=1, device_id={"dp": lax.rem(group + i, groups)}, device_id_type=pl.DeviceIdType.MESH)
        return _

    loop(1, n, greet, 0)
    loop(1, groups, greet_group, 0)

    def push(src, dst, send, recv, i, device):
        return pltpu.make_async_remote_copy(
            src_ref=src, dst_ref=dst, send_sem=send.at[i], recv_sem=recv.at[i],
            device_id={"blk": device}, device_id_type=pl.DeviceIdType.MESH)

    def kv_line(j):
        device = 2 * lax.rem(line + j, lines) + side
        return push(kv.at[0], kv.at[2 * j], kv_send, kv_recv, 2 * j, device)

    def kv_side(j):
        return push(kv.at[2 * j], kv.at[2 * j + 1], kv_send, kv_recv, 2 * j + 1, partner)

    def d_side(j):
        return push(xsend.at[j], xrecv.at[j], x_send, x_recv, j, partner)

    def d_line(j):
        device = 2 * lax.rem(line - j + lines, lines) + side
        return push(zsend.at[j], zrecv.at[j], z_send, z_recv, j, device)

    def g1_copy(i, slot):
        return pltpu.make_async_remote_copy(
            src_ref=gain1.at[slot], dst_ref=gain1.at[slot], send_sem=g1_send.at[i], recv_sem=g1_recv.at[i],
            device_id={"blk": lax.rem(me + i, n)}, device_id_type=pl.DeviceIdType.MESH)

    def g2_copy(i, slot):
        return pltpu.make_async_remote_copy(
            src_ref=gain2.at[slot], dst_ref=gain2.at[slot], send_sem=g2_send.at[i], recv_sem=g2_recv.at[i],
            device_id={"dp": lax.rem(group + i, groups)}, device_id_type=pl.DeviceIdType.MESH)

    for load in loads[:3]:
        load.wait()
    k_gain = kg_ref[...]
    k_float = k_ref[...].astype(F32)
    k_inv = lax.rsqrt(jnp.mean(k_float * k_float, axis=-1, keepdims=True) + EPSILON)
    kv[0, :, :hd] = (k_float * k_inv * k_gain).astype(BF16)

    pl.semaphore_wait(barrier, n - 1 + groups - 1)

    kv_side(0).start()

    def start_kv(j, _):
        kv_line(j).start()
        return _

    loop(1, lines, start_kv, 0)
    for load in loads[3:]:
        load.wait()
    q_gain = qg_ref[...]

    seq_length = len_ref[0]

    def positions(owner, axis, shape):
        ids = lax.broadcasted_iota(jnp.int32, shape, axis)
        first = order_ref[2 * owner] * half
        second = order_ref[2 * owner + 1] * half - half
        return ids + jnp.where(ids < half, first, second)

    q_pos = jnp.concatenate([positions(me, 1, (1, rows))] * heads, axis=1)
    live_lane = q_pos < seq_length
    live_rows = positions(me, 0, (rows, hd)) < seq_length
    q_invs = []
    g_cols = []
    for h in range(heads):
        cut = slice(h * hd, (h + 1) * hd)
        q_float = q_ref[:, cut].astype(F32)
        q_inv = lax.rsqrt(jnp.mean(q_float * q_float, axis=-1, keepdims=True) + EPSILON)
        q_invs.append(q_inv)
        q_hats[h * rows:(h + 1) * rows, :] = (q_float * q_inv * q_gain).astype(BF16)
        g_float = jnp.where(live_rows, go_ref[:, cut].astype(F32), 0.0)
        g_rows[h * rows:(h + 1) * rows, :] = g_float.astype(BF16)
        g_cols.append(jnp.transpose(g_float))
    g_cols = jnp.concatenate(g_cols, axis=1)

    def first_pass(i, top):
        k_pos = positions(owner_of(i), 0, (rows, heads * rows))
        k_pos = jnp.where(k_pos < seq_length, k_pos, FAR)
        s = dot_nt(kv[i, :, :hd], q_hats[...]) * (scale * LOG2E)
        s = jnp.where(k_pos <= q_pos, s, MASKED)
        score[i] = s
        pgrad[i] = dot_nt(kv[i, :, hd:], g_rows[...])
        return jnp.maximum(top, jnp.max(s, axis=0, keepdims=True))

    def first_pass_remote(j, top):
        kv_line(j).wait_recv()
        kv_side(j).start()
        top = first_pass(2 * j, top)
        kv_side(j - 1).wait_recv()
        return first_pass(2 * j - 1, top)

    top = first_pass(0, jnp.full((1, heads * rows), MASKED, F32))
    top = loop(1, lines, first_pass_remote, top)
    kv_side(lines - 1).wait_recv()
    top = first_pass(n - 1, top)

    def second_pass(i, carry):
        total, mixed = carry
        w = jnp.exp2(score[i] - top)
        score[i] = w
        total = total + jnp.sum(w, axis=0, keepdims=True)
        mixed = mixed + dot_tn(kv[i, :, hd:], w.astype(BF16))
        return total, mixed

    total, mixed = loop(
        0, n, second_pass,
        (jnp.zeros((1, heads * rows), F32), jnp.zeros((hd, heads * rows), F32)))
    inverse = 1.0 / total
    attended = jnp.where(live_lane, mixed * inverse, 0.0).astype(BF16).astype(F32)
    delta = jnp.sum(attended * g_cols, axis=0, keepdims=True)

    def third_pass(i, dq):
        p = score[i] * inverse
        ds = (p * (pgrad[i] - delta) * scale).astype(BF16)
        dk = dot_nn(ds, q_hats[...])
        dv = dot_nn(p.astype(BF16), g_rows[...])
        dq = dq + dot_tn(kv[i, :, :hd], ds)
        return dq, dk, dv

    def other_side(step, dq):
        j = (step + 1) % lines
        dq, dk, dv = third_pass(2 * j + 1, dq)
        xsend[j, :, :hd] = dk.astype(BF16)
        xsend[j, :, hd:] = dv.astype(BF16)
        d_side(j).start()
        return dq

    def own_side(j, dq):
        dq, dk, dv = third_pass(2 * j, dq)
        d_side(j).wait_recv()
        zsend[j, :, :hd] = (dk + xrecv[j, :, :hd].astype(F32)).astype(BF16)
        zsend[j, :, hd:] = (dv + xrecv[j, :, hd:].astype(F32)).astype(BF16)
        d_line(j).start()
        return dq

    dq = loop(0, lines, other_side, jnp.zeros((hd, heads * rows), F32))
    dq = loop(1, lines, own_side, dq)
    dq, dk, dv = third_pass(0, dq)

    part_q = jnp.zeros((1, hd), F32)
    part_k = jnp.zeros((1, hd), F32)
    dq_rows = []
    for h in range(heads):
        cut = slice(h * hd, (h + 1) * hd)
        dq_h = jnp.transpose(dq[:, h * rows:(h + 1) * rows])
        dq_rows.append(dq_h)
        q_float = q_ref[:, cut].astype(F32)
        part_q = part_q + jnp.sum(dq_h * q_float * q_invs[h], axis=0, keepdims=True)
        q_hat = q_hats[h * rows:(h + 1) * rows, :].astype(F32)
        part_k = part_k + jnp.sum(dq_h * q_hat, axis=0, keepdims=True)
    gain1[me, 0:1, :] = part_q
    gain1[me, 1:2, :] = part_k / k_gain

    def start_g1(i, _):
        g1_copy(i, me).start()
        return _

    loop(1, n, start_g1, 0)

    for h in range(heads):
        cut = slice(h * hd, (h + 1) * hd)
        q_float = q_ref[:, cut].astype(F32)
        q_inv = q_invs[h]
        scaled = q_gain * dq_rows[h]
        inner = jnp.mean(q_float * scaled, axis=-1, keepdims=True)
        qgrad_ref[:, cut] = (q_inv * scaled - q_float * (q_inv * q_inv * q_inv * inner)).astype(BF16)
        att_ref[:, cut] = jnp.transpose(attended[:, h * rows:(h + 1) * rows]).astype(BF16)

    stores[0].start()
    stores[1].start()

    def wait_g1(i, _):
        g1_copy(i, lax.rem(me - i + n, n)).wait_recv()
        return _

    loop(1, n, wait_g1, 0)
    gain2[group] = loop(1, n, lambda i, acc: acc + gain1[i], gain1[0])

    def start_g2(i, _):
        g2_copy(i, group).start()
        return _

    loop(1, groups, start_g2, 0)

    d_side(0).wait_recv()
    dk = dk + xrecv[0, :, :hd].astype(F32)
    dv = dv + xrecv[0, :, hd:].astype(F32)

    def gather(j, carry):
        dk, dv = carry
        d_line(j).wait_recv()
        return dk + zrecv[j, :, :hd].astype(F32), dv + zrecv[j, :, hd:].astype(F32)

    dk, dv = loop(1, lines, gather, (dk, dv))
    vgrad_ref[...] = dv.astype(BF16)
    stores[2].start()
    scaled = k_gain * dk
    inner = jnp.mean(k_float * scaled, axis=-1, keepdims=True)
    kgrad_ref[...] = (k_inv * scaled - k_float * (k_inv * k_inv * k_inv * inner)).astype(BF16)

    stores[3].start()

    def wait_g2(i, _):
        g2_copy(i, lax.rem(group - i + groups, groups)).wait_recv()
        return _

    loop(1, groups, wait_g2, 0)
    gains = loop(1, groups, lambda i, acc: acc + gain2[i], gain2[0])
    qgain_ref[...] = gains[0:1, :]
    kgain_ref[...] = gains[1:2, :]
    stores[4].start()
    stores[5].start()

    def drain(i, _):
        g1_copy(i, me).wait_send()
        return _

    loop(1, n, drain, 0)

    def drain_side(j, _):
        kv_side(j).wait_send()
        d_side(j).wait_send()
        return _

    def drain_line(j, _):
        kv_line(j).wait_send()
        d_line(j).wait_send()
        return _

    loop(0, lines, drain_side, 0)
    loop(1, lines, drain_line, 0)

    def drain_group(i, _):
        g2_copy(i, group).wait_send()
        return _

    loop(1, groups, drain_group, 0)
    for store in stores:
        store.wait()


def store_kernel(*refs):
    count = (len(refs) - 2) // 3
    sources, targets, held = refs[:count], refs[count:2 * count], refs[2 * count:3 * count]
    in_sem, out_sem = refs[3 * count:]
    loads = [pltpu.make_async_copy(sources[i], held[i], in_sem.at[i]) for i in range(count)]
    stores = [pltpu.make_async_copy(held[i], targets[i], out_sem.at[i]) for i in range(count)]
    for load in loads:
        load.start()
    for load, store in zip(loads, stores):
        load.wait()
        store.start()
    for store in stores:
        store.wait()


def per_device(n, groups, q_raw, k_raw, values, out_grad, q_gain, k_gain, block_order, seq_len):
    rows, wide = q_raw.shape[1:]
    hd = k_raw.shape[2]
    lanes = (wide // hd) * rows
    hbm = pl.BlockSpec(memory_space=pltpu.HBM)
    smem = pl.BlockSpec(memory_space=pltpu.SMEM)
    dma = pltpu.SemaphoreType.DMA
    out = pl.pallas_call(
        functools.partial(kernel, n, groups),
        out_shape=[
            jax.ShapeDtypeStruct((rows, wide), BF16),
            jax.ShapeDtypeStruct((rows, wide), BF16),
            jax.ShapeDtypeStruct((rows, hd), BF16),
            jax.ShapeDtypeStruct((rows, hd), BF16),
            jax.ShapeDtypeStruct((1, hd), F32),
            jax.ShapeDtypeStruct((1, hd), F32),
        ],
        in_specs=[smem, smem] + [hbm] * 6,
        out_specs=[hbm] * 6,
        scratch_shapes=[
            pltpu.VMEM((rows, wide), BF16),
            pltpu.VMEM((rows, hd), BF16),
            pltpu.VMEM((rows, wide), BF16),
            pltpu.VMEM((1, hd), F32),
            pltpu.VMEM((1, hd), F32),
            dma((6,)),
            pltpu.VMEM((rows, wide), BF16),
            pltpu.VMEM((rows, wide), BF16),
            pltpu.VMEM((rows, hd), BF16),
            pltpu.VMEM((rows, hd), BF16),
            pltpu.VMEM((1, hd), F32),
            pltpu.VMEM((1, hd), F32),
            dma((6,)),
            pltpu.VMEM((n, rows, 2 * hd), BF16),
            pltpu.VMEM((n, rows, lanes), F32),
            pltpu.VMEM((n, rows, lanes), F32),
            pltpu.VMEM((n // 2, rows, 2 * hd), BF16),
            pltpu.VMEM((n // 2, rows, 2 * hd), BF16),
            pltpu.VMEM((n // 2, rows, 2 * hd), BF16),
            pltpu.VMEM((n // 2, rows, 2 * hd), BF16),
            pltpu.VMEM((n, 2, hd), F32),
            pltpu.VMEM((groups, 2, hd), F32),
            pltpu.VMEM((lanes, hd), BF16),
            pltpu.VMEM((lanes, hd), BF16),
            dma((n,)), dma((n,)),
            dma((n // 2,)), dma((n // 2,)), dma((n // 2,)), dma((n // 2,)),
            dma((n,)), dma((n,)), dma((groups,)), dma((groups,)),
        ],
        compiler_params=pltpu.CompilerParams(
            collective_id=0, has_side_effects=True,
            vmem_limit_bytes=60 * 2**20),
    )(
        block_order, seq_len, q_raw[0], k_raw[0], values[0], out_grad[0],
        q_gain[None], k_gain[None],
    )
    out = pl.pallas_call(
        store_kernel,
        out_shape=[jax.ShapeDtypeStruct(o.shape, o.dtype) for o in out],
        in_specs=[hbm] * len(out),
        out_specs=[hbm] * len(out),
        scratch_shapes=[pltpu.VMEM(o.shape, o.dtype) for o in out] + [dma((len(out),)), dma((len(out),))],
        compiler_params=pltpu.CompilerParams(vmem_limit_bytes=60 * 2**20),
    )(*out)
    attended, q_grad, k_grad, v_grad, q_gain_grad, k_gain_grad = out
    return (attended[None], q_grad[None], k_grad[None], v_grad[None], q_gain_grad[0], k_gain_grad[0])


def solution(mesh):
    tokens = P("dp", "blk", None)
    in_specs = (tokens, tokens, tokens, tokens, P(), P(), P(), P("dp"))
    out_specs = (tokens, tokens, tokens, tokens, P(), P())
    return jax.shard_map(
        functools.partial(per_device, mesh.shape["blk"], mesh.shape["dp"]),
        mesh=mesh, in_specs=in_specs, out_specs=out_specs, check_vma=False)
```

```python
import functools

import jax
import jax.numpy as jnp
from jax import lax
from jax.experimental import pallas as pl
from jax.experimental.pallas import tpu as pltpu
from jax.sharding import PartitionSpec as P

EPSILON = 1e-06
MASKED = -1e30
FAR = 1 << 30
LOG2E = 1.4426950408889634
F32 = jnp.float32
BF16 = jnp.bfloat16


def loop(low, high, body, carry):
    if high - low <= 8:
        for i in range(low, high):
            carry = body(i, carry)
        return carry
    return lax.fori_loop(low, high, body, carry)


def dot_nt(a, b):
    return lax.dot_general(a, b, (((1,), (1,)), ((), ())), preferred_element_type=F32)


def dot_nn(a, b):
    return lax.dot_general(a, b, (((1,), (0,)), ((), ())), preferred_element_type=F32)


def dot_tn(a, b):
    return lax.dot_general(a, b, (((0,), (0,)), ((), ())), preferred_element_type=F32)


def kernel(
    n, groups, order_ref, len_ref, q_hbm, k_hbm, v_hbm, go_hbm, qg_hbm, kg_hbm,
    att_hbm, qgrad_hbm, kgrad_hbm, vgrad_hbm, qgain_hbm, kgain_hbm,
    q_ref, k_ref, go_ref, qg_ref, kg_ref, in_sem,
    att_ref, qgrad_ref, kgrad_ref, vgrad_ref, qgain_ref, kgain_ref, out_sem,
    kv, score, pgrad, xsend, xrecv, zsend, zrecv, gain1, gain2, q_hats, g_rows,
    kv_send, kv_recv, x_send, x_recv, z_send, z_recv, g1_send, g1_recv, g2_send, g2_recv,
):
    rows, hd = k_ref.shape
    heads = q_ref.shape[1] // hd
    half = rows // 2
    me = lax.axis_index("blk")
    group = lax.axis_index("dp")
    scale = hd ** (-0.5)
    lines = n // 2
    line, side = me // 2, lax.rem(me, 2)
    partner = 2 * line + 1 - side

    def owner_of(slot):
        other = lax.rem(side + slot // lines, 2)
        return 2 * lax.rem(line - slot % lines + lines, lines) + other

    loads = [
        pltpu.make_async_copy(src, dst, in_sem.at[i]) for i, (src, dst) in enumerate([
            (k_hbm, k_ref), (kg_hbm, kg_ref), (v_hbm, kv.at[0, :, pl.ds(hd, hd)]),
            (q_hbm, q_ref), (qg_hbm, qg_ref), (go_hbm, go_ref)])]
    for load in loads:
        load.start()

    stores = [
        pltpu.make_async_copy(src, dst, out_sem.at[i]) for i, (src, dst) in enumerate([
            (att_ref, att_hbm), (qgrad_ref, qgrad_hbm), (vgrad_ref, vgrad_hbm),
            (kgrad_ref, kgrad_hbm), (qgain_ref, qgain_hbm), (kgain_ref, kgain_hbm)])]

    barrier = pltpu.get_barrier_semaphore()

    def greet(i, _):
        pl.semaphore_signal(barrier, inc=1, device_id={"blk": lax.rem(me + i, n)}, device_id_type=pl.DeviceIdType.MESH)
        return _

    def greet_group(i, _):
        pl.semaphore_signal(barrier, inc=1, device_id={"dp": lax.rem(group + i, groups)}, device_id_type=pl.DeviceIdType.MESH)
        return _

    loop(1, n, greet, 0)
    loop(1, groups, greet_group, 0)

    def push(src, dst, send, recv, i, device):
        return pltpu.make_async_remote_copy(
            src_ref=src, dst_ref=dst, send_sem=send.at[i], recv_sem=recv.at[i],
            device_id={"blk": device}, device_id_type=pl.DeviceIdType.MESH)

    def kv_line(j):
        device = 2 * lax.rem(line + j, lines) + side
        return push(kv.at[0], kv.at[j], kv_send, kv_recv, j, device)

    def kv_side(j):
        return push(kv.at[j], kv.at[lines + j], kv_send, kv_recv, lines + j, partner)

    def d_side(j):
        return push(xsend.at[j], xrecv.at[j], x_send, x_recv, j, partner)

    def d_line(j):
        device = 2 * lax.rem(line - j + lines, lines) + side
        return push(zsend.at[j], zrecv.at[j], z_send, z_recv, j, device)

    def g1_copy(i, slot):
        return pltpu.make_async_remote_copy(
            src_ref=gain1.at[slot], dst_ref=gain1.at[slot], send_sem=g1_send.at[i], recv_sem=g1_recv.at[i],
            device_id={"blk": lax.rem(me + i, n)}, device_id_type=pl.DeviceIdType.MESH)

    def g2_copy(i, slot):
        return pltpu.make_async_remote_copy(
            src_ref=gain2.at[slot], dst_ref=gain2.at[slot], send_sem=g2_send.at[i], recv_sem=g2_recv.at[i],
            device_id={"dp": lax.rem(group + i, groups)}, device_id_type=pl.DeviceIdType.MESH)

    for load in loads[:3]:
        load.wait()
    k_gain = kg_ref[...]
    k_float = k_ref[...].astype(F32)
    k_inv = lax.rsqrt(jnp.mean(k_float * k_float, axis=-1, keepdims=True) + EPSILON)
    kv[0, :, :hd] = (k_float * k_inv * k_gain).astype(BF16)

    pl.semaphore_wait(barrier, n - 1 + groups - 1)

    kv_side(0).start()

    def start_kv(j, _):
        kv_line(j).start()
        return _

    loop(1, lines, start_kv, 0)
    for load in loads[3:]:
        load.wait()
    q_gain = qg_ref[...]

    seq_length = len_ref[0]

    def positions(owner, axis, shape):
        ids = lax.broadcasted_iota(jnp.int32, shape, axis)
        first = order_ref[2 * owner] * half
        second = order_ref[2 * owner + 1] * half - half
        return ids + jnp.where(ids < half, first, second)

    q_pos = jnp.concatenate([positions(me, 1, (1, rows))] * heads, axis=1)
    live_lane = q_pos < seq_length
    live_rows = positions(me, 0, (rows, hd)) < seq_length
    q_invs = []
    g_cols = []
    for h in range(heads):
        cut = slice(h * hd, (h + 1) * hd)
        q_float = q_ref[:, cut].astype(F32)
        q_inv = lax.rsqrt(jnp.mean(q_float * q_float, axis=-1, keepdims=True) + EPSILON)
        q_invs.append(q_inv)
        q_hats[h * rows:(h + 1) * rows, :] = (q_float * q_inv * q_gain).astype(BF16)
        g_float = jnp.where(live_rows, go_ref[:, cut].astype(F32), 0.0)
        g_rows[h * rows:(h + 1) * rows, :] = g_float.astype(BF16)
        g_cols.append(jnp.transpose(g_float))
    g_cols = jnp.concatenate(g_cols, axis=1)

    def first_pass(i, top):
        k_pos = positions(owner_of(i), 0, (rows, rows))
        k_pos = jnp.where(k_pos < seq_length, k_pos, FAR)
        bias = jnp.where(k_pos <= q_pos[:, :rows], 0.0, MASKED)
        s = dot_nt(kv[i, :, :hd], q_hats[...]) * (scale * LOG2E)
        s = s + jnp.concatenate([bias] * heads, axis=1)
        score[i] = s
        pgrad[i] = dot_nt(kv[i, :, hd:], g_rows[...])
        return jnp.maximum(top, jnp.max(s, axis=0, keepdims=True))

    def first_pass_remote(j, top):
        kv_line(j).wait_recv()
        kv_side(j).start()
        top = first_pass(j, top)
        kv_side(j - 1).wait_recv()
        return first_pass(lines + j - 1, top)

    top = first_pass(0, jnp.full((1, heads * rows), MASKED, F32))
    top = loop(1, lines, first_pass_remote, top)
    kv_side(lines - 1).wait_recv()
    top = first_pass(n - 1, top)

    def second_pass(p, carry):
        total, mixed = carry
        pair = pl.ds(2 * p, 2)
        w = jnp.exp2(score[pair].reshape(2 * rows, heads * rows) - top)
        score[pair] = w.reshape(2, rows, heads * rows)
        total = total + jnp.sum(w, axis=0, keepdims=True)
        mixed = mixed + dot_tn(kv[pair, :, hd:].reshape(2 * rows, hd), w.astype(BF16))
        return total, mixed

    total, mixed = loop(
        0, lines, second_pass,
        (jnp.zeros((1, heads * rows), F32), jnp.zeros((hd, heads * rows), F32)))
    inverse = 1.0 / total
    attended = jnp.where(live_lane, mixed * inverse, 0.0).astype(BF16).astype(F32)
    delta = jnp.sum(attended * g_cols, axis=0, keepdims=True)

    def third_pass(p, dq):
        pair = pl.ds(2 * p, 2)
        probs = score[pair].reshape(2 * rows, heads * rows) * inverse
        v_part = pgrad[pair].reshape(2 * rows, heads * rows)
        ds = (probs * (v_part - delta) * scale).astype(BF16)
        dk = dot_nn(ds, q_hats[...])
        dv = dot_nn(probs.astype(BF16), g_rows[...])
        dq = dq + dot_tn(kv[pair, :, :hd].reshape(2 * rows, hd), ds)
        return dq, dk, dv

    pairs = lines // 2

    def other_side(step, dq):
        p = (step + 1) % pairs
        dq, dk, dv = third_pass(pairs + p, dq)
        for e in range(2):
            j = 2 * p + e
            xsend[j, :, :hd] = dk[e * rows:(e + 1) * rows].astype(BF16)
            xsend[j, :, hd:] = dv[e * rows:(e + 1) * rows].astype(BF16)
            d_side(j).start()
        return dq

    def pass_on(j, dk, dv):
        d_side(j).wait_recv()
        zsend[j, :, :hd] = (dk + xrecv[j, :, :hd].astype(F32)).astype(BF16)
        zsend[j, :, hd:] = (dv + xrecv[j, :, hd:].astype(F32)).astype(BF16)
        d_line(j).start()

    def own_side(p, dq):
        dq, dk, dv = third_pass(p, dq)
        pass_on(2 * p, dk[:rows], dv[:rows])
        pass_on(2 * p + 1, dk[rows:], dv[rows:])
        return dq

    dq = loop(0, pairs, other_side, jnp.zeros((hd, heads * rows), F32))
    dq = loop(1, pairs, own_side, dq)
    dq, dk, dv = third_pass(0, dq)
    pass_on(1, dk[rows:], dv[rows:])
    dk, dv = dk[:rows], dv[:rows]

    part_q = jnp.zeros((1, hd), F32)
    part_k = jnp.zeros((1, hd), F32)
    dq_rows = []
    for h in range(heads):
        cut = slice(h * hd, (h + 1) * hd)
        dq_h = jnp.transpose(dq[:, h * rows:(h + 1) * rows])
        dq_rows.append(dq_h)
        q_float = q_ref[:, cut].astype(F32)
        part_q = part_q + jnp.sum(dq_h * q_float * q_invs[h], axis=0, keepdims=True)
        q_hat = q_hats[h * rows:(h + 1) * rows, :].astype(F32)
        part_k = part_k + jnp.sum(dq_h * q_hat, axis=0, keepdims=True)
    gain1[me, 0:1, :] = part_q
    gain1[me, 1:2, :] = part_k / k_gain

    def start_g1(i, _):
        g1_copy(i, me).start()
        return _

    loop(1, n, start_g1, 0)

    for h in range(heads):
        cut = slice(h * hd, (h + 1) * hd)
        q_float = q_ref[:, cut].astype(F32)
        q_inv = q_invs[h]
        scaled = q_gain * dq_rows[h]
        inner = jnp.mean(q_float * scaled, axis=-1, keepdims=True)
        qgrad_ref[:, cut] = (q_inv * scaled - q_float * (q_inv * q_inv * q_inv * inner)).astype(BF16)
        att_ref[:, cut] = jnp.transpose(attended[:, h * rows:(h + 1) * rows]).astype(BF16)

    stores[0].start()
    stores[1].start()

    def wait_g1(i, _):
        g1_copy(i, lax.rem(me - i + n, n)).wait_recv()
        return _

    loop(1, n, wait_g1, 0)
    gain2[group] = loop(1, n, lambda i, acc: acc + gain1[i], gain1[0])

    def start_g2(i, _):
        g2_copy(i, group).start()
        return _

    loop(1, groups, start_g2, 0)

    d_side(0).wait_recv()
    dk = dk + xrecv[0, :, :hd].astype(F32)
    dv = dv + xrecv[0, :, hd:].astype(F32)

    def gather(j, carry):
        dk, dv = carry
        d_line(j).wait_recv()
        return dk + zrecv[j, :, :hd].astype(F32), dv + zrecv[j, :, hd:].astype(F32)

    dk, dv = loop(1, lines, gather, (dk, dv))
    vgrad_ref[...] = dv.astype(BF16)
    stores[2].start()
    scaled = k_gain * dk
    inner = jnp.mean(k_float * scaled, axis=-1, keepdims=True)
    kgrad_ref[...] = (k_inv * scaled - k_float * (k_inv * k_inv * k_inv * inner)).astype(BF16)

    stores[3].start()

    def wait_g2(i, _):
        g2_copy(i, lax.rem(group - i + groups, groups)).wait_recv()
        return _

    loop(1, groups, wait_g2, 0)
    gains = loop(1, groups, lambda i, acc: acc + gain2[i], gain2[0])
    qgain_ref[...] = gains[0:1, :]
    kgain_ref[...] = gains[1:2, :]
    stores[4].start()
    stores[5].start()

    def drain(i, _):
        g1_copy(i, me).wait_send()
        return _

    loop(1, n, drain, 0)

    def drain_side(j, _):
        kv_side(j).wait_send()
        d_side(j).wait_send()
        return _

    def drain_line(j, _):
        kv_line(j).wait_send()
        d_line(j).wait_send()
        return _

    loop(0, lines, drain_side, 0)
    loop(1, lines, drain_line, 0)

    def drain_group(i, _):
        g2_copy(i, group).wait_send()
        return _

    loop(1, groups, drain_group, 0)
    for store in stores:
        store.wait()


def store_kernel(*refs):
    count = (len(refs) - 2) // 3
    sources, targets, held = refs[:count], refs[count:2 * count], refs[2 * count:3 * count]
    in_sem, out_sem = refs[3 * count:]
    loads = [pltpu.make_async_copy(sources[i], held[i], in_sem.at[i]) for i in range(count)]
    stores = [pltpu.make_async_copy(held[i], targets[i], out_sem.at[i]) for i in range(count)]
    for load in loads:
        load.start()
    for load, store in zip(loads, stores):
        load.wait()
        store.start()
    for store in stores:
        store.wait()


def per_device(n, groups, q_raw, k_raw, values, out_grad, q_gain, k_gain, block_order, seq_len):
    rows, wide = q_raw.shape[1:]
    hd = k_raw.shape[2]
    lanes = (wide // hd) * rows
    hbm = pl.BlockSpec(memory_space=pltpu.HBM)
    smem = pl.BlockSpec(memory_space=pltpu.SMEM)
    dma = pltpu.SemaphoreType.DMA
    out = pl.pallas_call(
        functools.partial(kernel, n, groups),
        out_shape=[
            jax.ShapeDtypeStruct((rows, wide), BF16),
            jax.ShapeDtypeStruct((rows, wide), BF16),
            jax.ShapeDtypeStruct((rows, hd), BF16),
            jax.ShapeDtypeStruct((rows, hd), BF16),
            jax.ShapeDtypeStruct((1, hd), F32),
            jax.ShapeDtypeStruct((1, hd), F32),
        ],
        in_specs=[smem, smem] + [hbm] * 6,
        out_specs=[hbm] * 6,
        scratch_shapes=[
            pltpu.VMEM((rows, wide), BF16),
            pltpu.VMEM((rows, hd), BF16),
            pltpu.VMEM((rows, wide), BF16),
            pltpu.VMEM((1, hd), F32),
            pltpu.VMEM((1, hd), F32),
            dma((6,)),
            pltpu.VMEM((rows, wide), BF16),
            pltpu.VMEM((rows, wide), BF16),
            pltpu.VMEM((rows, hd), BF16),
            pltpu.VMEM((rows, hd), BF16),
            pltpu.VMEM((1, hd), F32),
            pltpu.VMEM((1, hd), F32),
            dma((6,)),
            pltpu.VMEM((n, rows, 2 * hd), BF16),
            pltpu.VMEM((n, rows, lanes), F32),
            pltpu.VMEM((n, rows, lanes), F32),
            pltpu.VMEM((n // 2, rows, 2 * hd), BF16),
            pltpu.VMEM((n // 2, rows, 2 * hd), BF16),
            pltpu.VMEM((n // 2, rows, 2 * hd), BF16),
            pltpu.VMEM((n // 2, rows, 2 * hd), BF16),
            pltpu.VMEM((n, 2, hd), F32),
            pltpu.VMEM((groups, 2, hd), F32),
            pltpu.VMEM((lanes, hd), BF16),
            pltpu.VMEM((lanes, hd), BF16),
            dma((n,)), dma((n,)),
            dma((n // 2,)), dma((n // 2,)), dma((n // 2,)), dma((n // 2,)),
            dma((n,)), dma((n,)), dma((groups,)), dma((groups,)),
        ],
        compiler_params=pltpu.CompilerParams(
            collective_id=0, has_side_effects=True,
            vmem_limit_bytes=60 * 2**20),
    )(
        block_order, seq_len, q_raw[0], k_raw[0], values[0], out_grad[0],
        q_gain[None], k_gain[None],
    )
    out = pl.pallas_call(
        store_kernel,
        out_shape=[jax.ShapeDtypeStruct(o.shape, o.dtype) for o in out],
        in_specs=[hbm] * len(out),
        out_specs=[hbm] * len(out),
        scratch_shapes=[pltpu.VMEM(o.shape, o.dtype) for o in out] + [dma((len(out),)), dma((len(out),))],
        compiler_params=pltpu.CompilerParams(vmem_limit_bytes=60 * 2**20),
    )(*out)
    attended, q_grad, k_grad, v_grad, q_gain_grad, k_gain_grad = out
    return (attended[None], q_grad[None], k_grad[None], v_grad[None], q_gain_grad[0], k_gain_grad[0])


def solution(mesh):
    tokens = P("dp", "blk", None)
    in_specs = (tokens, tokens, tokens, tokens, P(), P(), P(), P("dp"))
    out_specs = (tokens, tokens, tokens, tokens, P(), P())
    return jax.shard_map(
        functools.partial(per_device, mesh.shape["blk"], mesh.shape["dp"]),
        mesh=mesh, in_specs=in_specs, out_specs=out_specs, check_vma=False)
```

```python
import functools

import jax
import jax.numpy as jnp
from jax import lax
from jax.experimental import pallas as pl
from jax.experimental.pallas import tpu as pltpu
from jax.sharding import PartitionSpec as P

EPSILON = 1e-06
MASKED = -1e30
FAR = 1 << 30
LOG2E = 1.4426950408889634
F32 = jnp.float32
BF16 = jnp.bfloat16


def loop(low, high, body, carry):
    if high - low <= 8:
        for i in range(low, high):
            carry = body(i, carry)
        return carry
    return lax.fori_loop(low, high, body, carry)


def dot_nt(a, b):
    return lax.dot_general(a, b, (((1,), (1,)), ((), ())), preferred_element_type=F32)


def dot_nn(a, b):
    return lax.dot_general(a, b, (((1,), (0,)), ((), ())), preferred_element_type=F32)


def dot_tn(a, b):
    return lax.dot_general(a, b, (((0,), (0,)), ((), ())), preferred_element_type=F32)


def kernel(
    n, groups, order_ref, len_ref, q_hbm, k_hbm, v_hbm, go_hbm, qg_hbm, kg_hbm,
    att_hbm, qgrad_hbm, kgrad_hbm, vgrad_hbm, qgain_hbm, kgain_hbm,
    q_ref, k_ref, go_ref, qg_ref, kg_ref, in_sem,
    att_ref, qgrad_ref, kgrad_ref, vgrad_ref, qgain_ref, kgain_ref, out_sem,
    kv, score, pgrad, xsend, xrecv, zsend, zrecv, gain1, gain2, q_hats, g_rows,
    kv_send, kv_recv, x_send, x_recv, z_send, z_recv, g1_send, g1_recv, g2_send, g2_recv,
):
    rows, hd = k_ref.shape
    heads = q_ref.shape[1] // hd
    half = rows // 2
    me = lax.axis_index("blk")
    group = lax.axis_index("dp")
    scale = hd ** (-0.5)
    lines = n // 2
    line, side = me // 2, lax.rem(me, 2)
    partner = 2 * line + 1 - side

    def owner_of(slot):
        other = lax.rem(side + slot // lines, 2)
        return 2 * lax.rem(line - slot % lines + lines, lines) + other

    loads = [
        pltpu.make_async_copy(src, dst, in_sem.at[i]) for i, (src, dst) in enumerate([
            (k_hbm, k_ref), (kg_hbm, kg_ref), (v_hbm, kv.at[0, :, pl.ds(hd, hd)]),
            (q_hbm, q_ref), (qg_hbm, qg_ref), (go_hbm, go_ref)])]
    for load in loads:
        load.start()

    stores = [
        pltpu.make_async_copy(src, dst, out_sem.at[i]) for i, (src, dst) in enumerate([
            (att_ref, att_hbm), (qgrad_ref, qgrad_hbm), (vgrad_ref, vgrad_hbm),
            (kgrad_ref, kgrad_hbm), (qgain_ref, qgain_hbm), (kgain_ref, kgain_hbm)])]

    barrier = pltpu.get_barrier_semaphore()

    def greet(i, _):
        pl.semaphore_signal(barrier, inc=1, device_id={"blk": lax.rem(me + i, n)}, device_id_type=pl.DeviceIdType.MESH)
        return _

    def greet_group(i, _):
        pl.semaphore_signal(barrier, inc=1, device_id={"dp": lax.rem(group + i, groups)}, device_id_type=pl.DeviceIdType.MESH)
        return _

    loop(1, n, greet, 0)
    loop(1, groups, greet_group, 0)

    def push(src, dst, send, recv, i, device):
        return pltpu.make_async_remote_copy(
            src_ref=src, dst_ref=dst, send_sem=send.at[i], recv_sem=recv.at[i],
            device_id={"blk": device}, device_id_type=pl.DeviceIdType.MESH)

    def piece(slot, part):
        return kv.at[slot, :, pl.ds(part * hd, hd)]

    def kv_line(j, part):
        device = 2 * lax.rem(line + j, lines) + side
        return push(piece(0, part), piece(j, part), kv_send, kv_recv, part * n + j, device)

    def kv_side(j, part):
        return push(piece(j, part), piece(lines + j, part), kv_send, kv_recv, part * n + lines + j, partner)

    def d_side(j):
        return push(xsend.at[j], xrecv.at[j], x_send, x_recv, j, partner)

    def d_line(j):
        device = 2 * lax.rem(line - j + lines, lines) + side
        return push(zsend.at[j], zrecv.at[j], z_send, z_recv, j, device)

    def g1_copy(i, slot):
        return pltpu.make_async_remote_copy(
            src_ref=gain1.at[slot], dst_ref=gain1.at[slot], send_sem=g1_send.at[i], recv_sem=g1_recv.at[i],
            device_id={"blk": lax.rem(me + i, n)}, device_id_type=pl.DeviceIdType.MESH)

    def g2_copy(i, slot):
        return pltpu.make_async_remote_copy(
            src_ref=gain2.at[slot], dst_ref=gain2.at[slot], send_sem=g2_send.at[i], recv_sem=g2_recv.at[i],
            device_id={"dp": lax.rem(group + i, groups)}, device_id_type=pl.DeviceIdType.MESH)

    for load in loads[:2]:
        load.wait()
    k_gain = kg_ref[...]
    k_float = k_ref[...].astype(F32)
    k_inv = lax.rsqrt(jnp.mean(k_float * k_float, axis=-1, keepdims=True) + EPSILON)
    kv[0, :, :hd] = (k_float * k_inv * k_gain).astype(BF16)

    pl.semaphore_wait(barrier, n - 1 + groups - 1)

    def start_kv(part):
        kv_side(0, part).start()

        def start_line(j, _):
            kv_line(j, part).start()
            return _

        loop(1, lines, start_line, 0)

    start_kv(0)
    loads[2].wait()
    start_kv(1)
    for load in loads[3:]:
        load.wait()
    q_gain = qg_ref[...]

    seq_length = len_ref[0]

    def positions(owner, axis, shape):
        ids = lax.broadcasted_iota(jnp.int32, shape, axis)
        first = order_ref[2 * owner] * half
        second = order_ref[2 * owner + 1] * half - half
        return ids + jnp.where(ids < half, first, second)

    q_pos = jnp.concatenate([positions(me, 1, (1, rows))] * heads, axis=1)
    live_lane = q_pos < seq_length
    live_rows = positions(me, 0, (rows, hd)) < seq_length
    q_invs = []
    g_cols = []
    for h in range(heads):
        cut = slice(h * hd, (h + 1) * hd)
        q_float = q_ref[:, cut].astype(F32)
        q_inv = lax.rsqrt(jnp.mean(q_float * q_float, axis=-1, keepdims=True) + EPSILON)
        q_invs.append(q_inv)
        q_hats[h * rows:(h + 1) * rows, :] = (q_float * q_inv * q_gain).astype(BF16)
        g_float = jnp.where(live_rows, go_ref[:, cut].astype(F32), 0.0)
        g_rows[h * rows:(h + 1) * rows, :] = g_float.astype(BF16)
        g_cols.append(jnp.transpose(g_float))
    g_cols = jnp.concatenate(g_cols, axis=1)

    def first_pass(i, top):
        k_pos = positions(owner_of(i), 0, (rows, rows))
        k_pos = jnp.where(k_pos < seq_length, k_pos, FAR)
        bias = jnp.where(k_pos <= q_pos[:, :rows], 0.0, MASKED)
        s = dot_nt(kv[i, :, :hd], q_hats[...]) * (scale * LOG2E)
        s = s + jnp.concatenate([bias] * heads, axis=1)
        score[i] = s
        return jnp.maximum(top, jnp.max(s, axis=0, keepdims=True))

    def value_pass(i, carry):
        pgrad[i] = dot_nt(kv[i, :, hd:], g_rows[...])
        return carry

    def arrivals(part, work, carry):
        def step(j, carry):
            kv_line(j, part).wait_recv()
            kv_side(j, part).start()
            carry = work(j, carry)
            kv_side(j - 1, part).wait_recv()
            return work(lines + j - 1, carry)

        carry = work(0, carry)
        carry = loop(1, lines, step, carry)
        kv_side(lines - 1, part).wait_recv()
        return work(n - 1, carry)

    top = arrivals(0, first_pass, jnp.full((1, heads * rows), MASKED, F32))
    arrivals(1, value_pass, 0)

    def second_pass(p, carry):
        total, mixed = carry
        pair = pl.ds(2 * p, 2)
        w = jnp.exp2(score[pair].reshape(2 * rows, heads * rows) - top)
        score[pair] = w.reshape(2, rows, heads * rows)
        total = total + jnp.sum(w, axis=0, keepdims=True)
        mixed = mixed + dot_tn(kv[pair, :, hd:].reshape(2 * rows, hd), w.astype(BF16))
        return total, mixed

    total, mixed = loop(
        0, lines, second_pass,
        (jnp.zeros((1, heads * rows), F32), jnp.zeros((hd, heads * rows), F32)))
    inverse = 1.0 / total
    attended = jnp.where(live_lane, mixed * inverse, 0.0).astype(BF16).astype(F32)
    delta = jnp.sum(attended * g_cols, axis=0, keepdims=True)

    def third_pass(p, dq):
        pair = pl.ds(2 * p, 2)
        probs = score[pair].reshape(2 * rows, heads * rows) * inverse
        v_part = pgrad[pair].reshape(2 * rows, heads * rows)
        ds = (probs * (v_part - delta) * scale).astype(BF16)
        dk = dot_nn(ds, q_hats[...])
        dv = dot_nn(probs.astype(BF16), g_rows[...])
        dq = dq + dot_tn(kv[pair, :, :hd].reshape(2 * rows, hd), ds)
        return dq, dk, dv

    pairs = lines // 2

    def other_side(step, dq):
        p = (step + 1) % pairs
        dq, dk, dv = third_pass(pairs + p, dq)
        for e in range(2):
            j = 2 * p + e
            xsend[j, :, :hd] = dk[e * rows:(e + 1) * rows].astype(BF16)
            xsend[j, :, hd:] = dv[e * rows:(e + 1) * rows].astype(BF16)
            d_side(j).start()
        return dq

    def pass_on(j, dk, dv):
        d_side(j).wait_recv()
        zsend[j, :, :hd] = (dk + xrecv[j, :, :hd].astype(F32)).astype(BF16)
        zsend[j, :, hd:] = (dv + xrecv[j, :, hd:].astype(F32)).astype(BF16)
        d_line(j).start()

    def own_side(p, dq):
        dq, dk, dv = third_pass(p, dq)
        pass_on(2 * p, dk[:rows], dv[:rows])
        pass_on(2 * p + 1, dk[rows:], dv[rows:])
        return dq

    dq = loop(0, pairs, other_side, jnp.zeros((hd, heads * rows), F32))
    dq = loop(1, pairs, own_side, dq)
    dq, dk, dv = third_pass(0, dq)
    pass_on(1, dk[rows:], dv[rows:])
    dk, dv = dk[:rows], dv[:rows]

    part_q = jnp.zeros((1, hd), F32)
    part_k = jnp.zeros((1, hd), F32)
    dq_rows = []
    for h in range(heads):
        cut = slice(h * hd, (h + 1) * hd)
        dq_h = jnp.transpose(dq[:, h * rows:(h + 1) * rows])
        dq_rows.append(dq_h)
        q_float = q_ref[:, cut].astype(F32)
        part_q = part_q + jnp.sum(dq_h * q_float * q_invs[h], axis=0, keepdims=True)
        q_hat = q_hats[h * rows:(h + 1) * rows, :].astype(F32)
        part_k = part_k + jnp.sum(dq_h * q_hat, axis=0, keepdims=True)
    gain1[me, 0:1, :] = part_q
    gain1[me, 1:2, :] = part_k / k_gain

    def start_g1(i, _):
        g1_copy(i, me).start()
        return _

    loop(1, n, start_g1, 0)

    for h in range(heads):
        cut = slice(h * hd, (h + 1) * hd)
        q_float = q_ref[:, cut].astype(F32)
        q_inv = q_invs[h]
        scaled = q_gain * dq_rows[h]
        inner = jnp.mean(q_float * scaled, axis=-1, keepdims=True)
        qgrad_ref[:, cut] = (q_inv * scaled - q_float * (q_inv * q_inv * q_inv * inner)).astype(BF16)
        att_ref[:, cut] = jnp.transpose(attended[:, h * rows:(h + 1) * rows]).astype(BF16)

    stores[0].start()
    stores[1].start()

    def wait_g1(i, _):
        g1_copy(i, lax.rem(me - i + n, n)).wait_recv()
        return _

    loop(1, n, wait_g1, 0)
    gain2[group] = loop(1, n, lambda i, acc: acc + gain1[i], gain1[0])

    def start_g2(i, _):
        g2_copy(i, group).start()
        return _

    loop(1, groups, start_g2, 0)

    d_side(0).wait_recv()
    dk = dk + xrecv[0, :, :hd].astype(F32)
    dv = dv + xrecv[0, :, hd:].astype(F32)

    def gather(j, carry):
        dk, dv = carry
        d_line(j).wait_recv()
        return dk + zrecv[j, :, :hd].astype(F32), dv + zrecv[j, :, hd:].astype(F32)

    dk, dv = loop(1, lines, gather, (dk, dv))
    vgrad_ref[...] = dv.astype(BF16)
    stores[2].start()
    scaled = k_gain * dk
    inner = jnp.mean(k_float * scaled, axis=-1, keepdims=True)
    kgrad_ref[...] = (k_inv * scaled - k_float * (k_inv * k_inv * k_inv * inner)).astype(BF16)

    stores[3].start()

    def wait_g2(i, _):
        g2_copy(i, lax.rem(group - i + groups, groups)).wait_recv()
        return _

    loop(1, groups, wait_g2, 0)
    gains = loop(1, groups, lambda i, acc: acc + gain2[i], gain2[0])
    qgain_ref[...] = gains[0:1, :]
    kgain_ref[...] = gains[1:2, :]
    stores[4].start()
    stores[5].start()

    def drain(i, _):
        g1_copy(i, me).wait_send()
        return _

    loop(1, n, drain, 0)

    def drain_side(j, _):
        kv_side(j, 0).wait_send()
        kv_side(j, 1).wait_send()
        d_side(j).wait_send()
        return _

    def drain_line(j, _):
        kv_line(j, 0).wait_send()
        kv_line(j, 1).wait_send()
        d_line(j).wait_send()
        return _

    loop(0, lines, drain_side, 0)
    loop(1, lines, drain_line, 0)

    def drain_group(i, _):
        g2_copy(i, group).wait_send()
        return _

    loop(1, groups, drain_group, 0)
    for store in stores:
        store.wait()


def store_kernel(*refs):
    count = (len(refs) - 2) // 3
    sources, targets, held = refs[:count], refs[count:2 * count], refs[2 * count:3 * count]
    in_sem, out_sem = refs[3 * count:]
    loads = [pltpu.make_async_copy(sources[i], held[i], in_sem.at[i]) for i in range(count)]
    stores = [pltpu.make_async_copy(held[i], targets[i], out_sem.at[i]) for i in range(count)]
    for load in loads:
        load.start()
    for load, store in zip(loads, stores):
        load.wait()
        store.start()
    for store in stores:
        store.wait()


def per_device(n, groups, q_raw, k_raw, values, out_grad, q_gain, k_gain, block_order, seq_len):
    rows, wide = q_raw.shape[1:]
    hd = k_raw.shape[2]
    lanes = (wide // hd) * rows
    hbm = pl.BlockSpec(memory_space=pltpu.HBM)
    smem = pl.BlockSpec(memory_space=pltpu.SMEM)
    dma = pltpu.SemaphoreType.DMA
    out = pl.pallas_call(
        functools.partial(kernel, n, groups),
        out_shape=[
            jax.ShapeDtypeStruct((rows, wide), BF16),
            jax.ShapeDtypeStruct((rows, wide), BF16),
            jax.ShapeDtypeStruct((rows, hd), BF16),
            jax.ShapeDtypeStruct((rows, hd), BF16),
            jax.ShapeDtypeStruct((1, hd), F32),
            jax.ShapeDtypeStruct((1, hd), F32),
        ],
        in_specs=[smem, smem] + [hbm] * 6,
        out_specs=[hbm] * 6,
        scratch_shapes=[
            pltpu.VMEM((rows, wide), BF16),
            pltpu.VMEM((rows, hd), BF16),
            pltpu.VMEM((rows, wide), BF16),
            pltpu.VMEM((1, hd), F32),
            pltpu.VMEM((1, hd), F32),
            dma((6,)),
            pltpu.VMEM((rows, wide), BF16),
            pltpu.VMEM((rows, wide), BF16),
            pltpu.VMEM((rows, hd), BF16),
            pltpu.VMEM((rows, hd), BF16),
            pltpu.VMEM((1, hd), F32),
            pltpu.VMEM((1, hd), F32),
            dma((6,)),
            pltpu.VMEM((n, rows, 2 * hd), BF16),
            pltpu.VMEM((n, rows, lanes), F32),
            pltpu.VMEM((n, rows, lanes), F32),
            pltpu.VMEM((n // 2, rows, 2 * hd), BF16),
            pltpu.VMEM((n // 2, rows, 2 * hd), BF16),
            pltpu.VMEM((n // 2, rows, 2 * hd), BF16),
            pltpu.VMEM((n // 2, rows, 2 * hd), BF16),
            pltpu.VMEM((n, 2, hd), F32),
            pltpu.VMEM((groups, 2, hd), F32),
            pltpu.VMEM((lanes, hd), BF16),
            pltpu.VMEM((lanes, hd), BF16),
            dma((2 * n,)), dma((2 * n,)),
            dma((n // 2,)), dma((n // 2,)), dma((n // 2,)), dma((n // 2,)),
            dma((n,)), dma((n,)), dma((groups,)), dma((groups,)),
        ],
        compiler_params=pltpu.CompilerParams(
            collective_id=0, has_side_effects=True,
            vmem_limit_bytes=60 * 2**20),
    )(
        block_order, seq_len, q_raw[0], k_raw[0], values[0], out_grad[0],
        q_gain[None], k_gain[None],
    )
    out = pl.pallas_call(
        store_kernel,
        out_shape=[jax.ShapeDtypeStruct(o.shape, o.dtype) for o in out],
        in_specs=[hbm] * len(out),
        out_specs=[hbm] * len(out),
        scratch_shapes=[pltpu.VMEM(o.shape, o.dtype) for o in out] + [dma((len(out),)), dma((len(out),))],
        compiler_params=pltpu.CompilerParams(vmem_limit_bytes=60 * 2**20),
    )(*out)
    attended, q_grad, k_grad, v_grad, q_gain_grad, k_gain_grad = out
    return (attended[None], q_grad[None], k_grad[None], v_grad[None], q_gain_grad[0], k_gain_grad[0])


def solution(mesh):
    tokens = P("dp", "blk", None)
    in_specs = (tokens, tokens, tokens, tokens, P(), P(), P(), P("dp"))
    out_specs = (tokens, tokens, tokens, tokens, P(), P())
    return jax.shard_map(
        functools.partial(per_device, mesh.shape["blk"], mesh.shape["dp"]),
        mesh=mesh, in_specs=in_specs, out_specs=out_specs, check_vma=False)
```

```python
import functools

import jax
import jax.numpy as jnp
from jax import lax
from jax.experimental import pallas as pl
from jax.experimental.pallas import tpu as pltpu
from jax.sharding import PartitionSpec as P

EPSILON = 1e-06
MASKED = -1e30
FAR = 1 << 30
LOG2E = 1.4426950408889634
F32 = jnp.float32
BF16 = jnp.bfloat16


def loop(low, high, body, carry):
    if high - low <= 8:
        for i in range(low, high):
            carry = body(i, carry)
        return carry
    return lax.fori_loop(low, high, body, carry)


def dot_nt(a, b):
    return lax.dot_general(a, b, (((1,), (1,)), ((), ())), preferred_element_type=F32)


def dot_nn(a, b):
    return lax.dot_general(a, b, (((1,), (0,)), ((), ())), preferred_element_type=F32)


def dot_tn(a, b):
    return lax.dot_general(a, b, (((0,), (0,)), ((), ())), preferred_element_type=F32)


def kernel(
    n, groups, order_ref, len_ref, q_hbm, k_hbm, v_hbm, go_hbm, qg_hbm, kg_hbm,
    att_hbm, qgrad_hbm, kgrad_hbm, vgrad_hbm, qgain_hbm, kgain_hbm,
    q_ref, k_ref, go_ref, qg_ref, kg_ref, in_sem,
    att_ref, qgrad_ref, kgrad_ref, vgrad_ref, qgain_ref, kgain_ref, out_sem,
    kv, score, pgrad, xsend, xrecv, zsend, zrecv, gain1, gain2, q_hats, g_rows,
    kv_send, kv_recv, x_send, x_recv, z_send, z_recv, g1_send, g1_recv, g2_send, g2_recv,
):
    rows, hd = k_ref.shape
    heads = q_ref.shape[1] // hd
    half = rows // 2
    me = lax.axis_index("blk")
    group = lax.axis_index("dp")
    scale = hd ** (-0.5)
    lines = n // 2
    line, side = me // 2, lax.rem(me, 2)
    partner = 2 * line + 1 - side

    def owner_of(slot):
        other = lax.rem(side + slot // lines, 2)
        return 2 * lax.rem(line - slot % lines + lines, lines) + other

    loads = [
        pltpu.make_async_copy(src, dst, in_sem.at[i]) for i, (src, dst) in enumerate([
            (k_hbm, k_ref), (kg_hbm, kg_ref), (v_hbm, kv.at[0, :, pl.ds(hd, hd)]),
            (q_hbm, q_ref), (qg_hbm, qg_ref), (go_hbm, go_ref)])]
    for load in loads:
        load.start()

    stores = [
        pltpu.make_async_copy(src, dst, out_sem.at[i]) for i, (src, dst) in enumerate([
            (att_ref, att_hbm), (qgrad_ref, qgrad_hbm), (vgrad_ref, vgrad_hbm),
            (kgrad_ref, kgrad_hbm), (qgain_ref, qgain_hbm), (kgain_ref, kgain_hbm)])]

    barrier = pltpu.get_barrier_semaphore()

    def greet(i, _):
        pl.semaphore_signal(barrier, inc=1, device_id={"blk": lax.rem(me + i, n)}, device_id_type=pl.DeviceIdType.MESH)
        return _

    def greet_group(i, _):
        pl.semaphore_signal(barrier, inc=1, device_id={"dp": lax.rem(group + i, groups)}, device_id_type=pl.DeviceIdType.MESH)
        return _

    loop(1, n, greet, 0)
    loop(1, groups, greet_group, 0)

    def push(src, dst, send, recv, i, device):
        return pltpu.make_async_remote_copy(
            src_ref=src, dst_ref=dst, send_sem=send.at[i], recv_sem=recv.at[i],
            device_id={"blk": device}, device_id_type=pl.DeviceIdType.MESH)

    def kv_line(j):
        device = 2 * lax.rem(line + j, lines) + side
        return push(kv.at[0], kv.at[j], kv_send, kv_recv, j, device)

    def kv_side(j):
        return push(kv.at[j], kv.at[lines + j], kv_send, kv_recv, lines + j, partner)

    def d_side(j):
        return push(xsend.at[j], xrecv.at[j], x_send, x_recv, j, partner)

    def d_line(j):
        device = 2 * lax.rem(line - j + lines, lines) + side
        return push(zsend.at[j], zrecv.at[j], z_send, z_recv, j, device)

    def g1_copy(i, slot):
        return pltpu.make_async_remote_copy(
            src_ref=gain1.at[slot], dst_ref=gain1.at[slot], send_sem=g1_send.at[i], recv_sem=g1_recv.at[i],
            device_id={"blk": lax.rem(me + i, n)}, device_id_type=pl.DeviceIdType.MESH)

    def g2_copy(i, slot):
        return pltpu.make_async_remote_copy(
            src_ref=gain2.at[slot], dst_ref=gain2.at[slot], send_sem=g2_send.at[i], recv_sem=g2_recv.at[i],
            device_id={"dp": lax.rem(group + i, groups)}, device_id_type=pl.DeviceIdType.MESH)

    for load in loads[:3]:
        load.wait()
    k_gain = kg_ref[...]
    k_float = k_ref[...].astype(F32)
    k_inv = lax.rsqrt(jnp.mean(k_float * k_float, axis=-1, keepdims=True) + EPSILON)
    kv[0, :, :hd] = (k_float * k_inv * k_gain).astype(BF16)

    pl.semaphore_wait(barrier, n - 1 + groups - 1)

    kv_side(0).start()

    def turn(i):
        return 1 + (i - 1 + lines // 2 - 1) % (lines - 1)

    def start_kv(i, _):
        kv_line(turn(i)).start()
        return _

    loop(1, lines, start_kv, 0)
    for load in loads[3:]:
        load.wait()
    q_gain = qg_ref[...]

    seq_length = len_ref[0]

    def positions(owner, axis, shape):
        ids = lax.broadcasted_iota(jnp.int32, shape, axis)
        first = order_ref[2 * owner] * half
        second = order_ref[2 * owner + 1] * half - half
        return ids + jnp.where(ids < half, first, second)

    q_pos = jnp.concatenate([positions(me, 1, (1, rows))] * heads, axis=1)
    live_lane = q_pos < seq_length
    live_rows = positions(me, 0, (rows, hd)) < seq_length
    q_invs = []
    g_cols = []
    for h in range(heads):
        cut = slice(h * hd, (h + 1) * hd)
        q_float = q_ref[:, cut].astype(F32)
        q_inv = lax.rsqrt(jnp.mean(q_float * q_float, axis=-1, keepdims=True) + EPSILON)
        q_invs.append(q_inv)
        q_hats[h * rows:(h + 1) * rows, :] = (q_float * q_inv * q_gain).astype(BF16)
        g_float = jnp.where(live_rows, go_ref[:, cut].astype(F32), 0.0)
        g_rows[h * rows:(h + 1) * rows, :] = g_float.astype(BF16)
        g_cols.append(jnp.transpose(g_float))
    g_cols = jnp.concatenate(g_cols, axis=1)

    def first_pass(i, top):
        k_pos = positions(owner_of(i), 0, (rows, rows))
        k_pos = jnp.where(k_pos < seq_length, k_pos, FAR)
        bias = jnp.where(k_pos <= q_pos[:, :rows], 0.0, MASKED)
        s = dot_nt(kv[i, :, :hd], q_hats[...]) * (scale * LOG2E)
        s = s + jnp.concatenate([bias] * heads, axis=1)
        score[i] = s
        pgrad[i] = dot_nt(kv[i, :, hd:], g_rows[...])
        return jnp.maximum(top, jnp.max(s, axis=0, keepdims=True))

    def first_pass_remote(i, top):
        j = turn(i)
        before = turn(i - 1) * ((i + lines - 2) // lines)
        kv_line(j).wait_recv()
        kv_side(j).start()
        top = first_pass(j, top)
        kv_side(before).wait_recv()
        return first_pass(lines + before, top)

    top = first_pass(0, jnp.full((1, heads * rows), MASKED, F32))
    top = loop(1, lines, first_pass_remote, top)
    last = turn(lines - 1)
    kv_side(last).wait_recv()
    top = first_pass(lines + last, top)

    def second_pass(p, carry):
        total, mixed = carry
        pair = pl.ds(2 * p, 2)
        w = jnp.exp2(score[pair].reshape(2 * rows, heads * rows) - top)
        score[pair] = w.reshape(2, rows, heads * rows)
        total = total + jnp.sum(w, axis=0, keepdims=True)
        mixed = mixed + dot_tn(kv[pair, :, hd:].reshape(2 * rows, hd), w.astype(BF16))
        return total, mixed

    total, mixed = loop(
        0, lines, second_pass,
        (jnp.zeros((1, heads * rows), F32), jnp.zeros((hd, heads * rows), F32)))
    inverse = 1.0 / total
    attended = jnp.where(live_lane, mixed * inverse, 0.0).astype(BF16).astype(F32)
    delta = jnp.sum(attended * g_cols, axis=0, keepdims=True)

    def third_pass(p, dq):
        pair = pl.ds(2 * p, 2)
        probs = score[pair].reshape(2 * rows, heads * rows) * inverse
        v_part = pgrad[pair].reshape(2 * rows, heads * rows)
        ds = (probs * (v_part - delta) * scale).astype(BF16)
        dk = dot_nn(ds, q_hats[...])
        dv = dot_nn(probs.astype(BF16), g_rows[...])
        dq = dq + dot_tn(kv[pair, :, :hd].reshape(2 * rows, hd), ds)
        return dq, dk, dv

    pairs = lines // 2

    def other_side(step, dq):
        p = (step + 1) % pairs
        dq, dk, dv = third_pass(pairs + p, dq)
        for e in range(2):
            j = 2 * p + e
            xsend[j, :, :hd] = dk[e * rows:(e + 1) * rows].astype(BF16)
            xsend[j, :, hd:] = dv[e * rows:(e + 1) * rows].astype(BF16)
            d_side(j).start()
        return dq

    def pass_on(j, dk, dv):
        d_side(j).wait_recv()
        zsend[j, :, :hd] = (dk + xrecv[j, :, :hd].astype(F32)).astype(BF16)
        zsend[j, :, hd:] = (dv + xrecv[j, :, hd:].astype(F32)).astype(BF16)
        d_line(j).start()

    def own_side(p, dq):
        dq, dk, dv = third_pass(p, dq)
        pass_on(2 * p, dk[:rows], dv[:rows])
        pass_on(2 * p + 1, dk[rows:], dv[rows:])
        return dq

    dq = loop(0, pairs, other_side, jnp.zeros((hd, heads * rows), F32))
    dq = loop(1, pairs, own_side, dq)
    dq, dk, dv = third_pass(0, dq)
    pass_on(1, dk[rows:], dv[rows:])
    dk, dv = dk[:rows], dv[:rows]

    part_q = jnp.zeros((1, hd), F32)
    part_k = jnp.zeros((1, hd), F32)
    dq_rows = []
    for h in range(heads):
        cut = slice(h * hd, (h + 1) * hd)
        dq_h = jnp.transpose(dq[:, h * rows:(h + 1) * rows])
        dq_rows.append(dq_h)
        q_float = q_ref[:, cut].astype(F32)
        part_q = part_q + jnp.sum(dq_h * q_float * q_invs[h], axis=0, keepdims=True)
        q_hat = q_hats[h * rows:(h + 1) * rows, :].astype(F32)
        part_k = part_k + jnp.sum(dq_h * q_hat, axis=0, keepdims=True)
    gain1[me, 0:1, :] = part_q
    gain1[me, 1:2, :] = part_k / k_gain

    def start_g1(i, _):
        g1_copy(i, me).start()
        return _

    loop(1, n, start_g1, 0)

    for h in range(heads):
        cut = slice(h * hd, (h + 1) * hd)
        q_float = q_ref[:, cut].astype(F32)
        q_inv = q_invs[h]
        scaled = q_gain * dq_rows[h]
        inner = jnp.mean(q_float * scaled, axis=-1, keepdims=True)
        qgrad_ref[:, cut] = (q_inv * scaled - q_float * (q_inv * q_inv * q_inv * inner)).astype(BF16)
        att_ref[:, cut] = jnp.transpose(attended[:, h * rows:(h + 1) * rows]).astype(BF16)

    stores[0].start()
    stores[1].start()

    def wait_g1(i, _):
        g1_copy(i, lax.rem(me - i + n, n)).wait_recv()
        return _

    loop(1, n, wait_g1, 0)
    gain2[group] = loop(1, n, lambda i, acc: acc + gain1[i], gain1[0])

    def start_g2(i, _):
        g2_copy(i, group).start()
        return _

    loop(1, groups, start_g2, 0)

    d_side(0).wait_recv()
    dk = dk + xrecv[0, :, :hd].astype(F32)
    dv = dv + xrecv[0, :, hd:].astype(F32)

    def gather(j, carry):
        dk, dv = carry
        d_line(j).wait_recv()
        return dk + zrecv[j, :, :hd].astype(F32), dv + zrecv[j, :, hd:].astype(F32)

    dk, dv = loop(1, lines, gather, (dk, dv))
    vgrad_ref[...] = dv.astype(BF16)
    stores[2].start()
    scaled = k_gain * dk
    inner = jnp.mean(k_float * scaled, axis=-1, keepdims=True)
    kgrad_ref[...] = (k_inv * scaled - k_float * (k_inv * k_inv * k_inv * inner)).astype(BF16)

    stores[3].start()

    def wait_g2(i, _):
        g2_copy(i, lax.rem(group - i + groups, groups)).wait_recv()
        return _

    loop(1, groups, wait_g2, 0)
    gains = loop(1, groups, lambda i, acc: acc + gain2[i], gain2[0])
    qgain_ref[...] = gains[0:1, :]
    kgain_ref[...] = gains[1:2, :]
    stores[4].start()
    stores[5].start()

    def drain(i, _):
        g1_copy(i, me).wait_send()
        return _

    loop(1, n, drain, 0)

    def drain_side(j, _):
        kv_side(j).wait_send()
        d_side(j).wait_send()
        return _

    def drain_line(j, _):
        kv_line(j).wait_send()
        d_line(j).wait_send()
        return _

    loop(0, lines, drain_side, 0)
    loop(1, lines, drain_line, 0)

    def drain_group(i, _):
        g2_copy(i, group).wait_send()
        return _

    loop(1, groups, drain_group, 0)
    for store in stores:
        store.wait()


def store_kernel(*refs):
    count = (len(refs) - 2) // 3
    sources, targets, held = refs[:count], refs[count:2 * count], refs[2 * count:3 * count]
    in_sem, out_sem = refs[3 * count:]
    loads = [pltpu.make_async_copy(sources[i], held[i], in_sem.at[i]) for i in range(count)]
    stores = [pltpu.make_async_copy(held[i], targets[i], out_sem.at[i]) for i in range(count)]
    for load in loads:
        load.start()
    for load, store in zip(loads, stores):
        load.wait()
        store.start()
    for store in stores:
        store.wait()


def per_device(n, groups, q_raw, k_raw, values, out_grad, q_gain, k_gain, block_order, seq_len):
    rows, wide = q_raw.shape[1:]
    hd = k_raw.shape[2]
    lanes = (wide // hd) * rows
    hbm = pl.BlockSpec(memory_space=pltpu.HBM)
    smem = pl.BlockSpec(memory_space=pltpu.SMEM)
    dma = pltpu.SemaphoreType.DMA
    out = pl.pallas_call(
        functools.partial(kernel, n, groups),
        out_shape=[
            jax.ShapeDtypeStruct((rows, wide), BF16),
            jax.ShapeDtypeStruct((rows, wide), BF16),
            jax.ShapeDtypeStruct((rows, hd), BF16),
            jax.ShapeDtypeStruct((rows, hd), BF16),
            jax.ShapeDtypeStruct((1, hd), F32),
            jax.ShapeDtypeStruct((1, hd), F32),
        ],
        in_specs=[smem, smem] + [hbm] * 6,
        out_specs=[hbm] * 6,
        scratch_shapes=[
            pltpu.VMEM((rows, wide), BF16),
            pltpu.VMEM((rows, hd), BF16),
            pltpu.VMEM((rows, wide), BF16),
            pltpu.VMEM((1, hd), F32),
            pltpu.VMEM((1, hd), F32),
            dma((6,)),
            pltpu.VMEM((rows, wide), BF16),
            pltpu.VMEM((rows, wide), BF16),
            pltpu.VMEM((rows, hd), BF16),
            pltpu.VMEM((rows, hd), BF16),
            pltpu.VMEM((1, hd), F32),
            pltpu.VMEM((1, hd), F32),
            dma((6,)),
            pltpu.VMEM((n, rows, 2 * hd), BF16),
            pltpu.VMEM((n, rows, lanes), F32),
            pltpu.VMEM((n, rows, lanes), F32),
            pltpu.VMEM((n // 2, rows, 2 * hd), BF16),
            pltpu.VMEM((n // 2, rows, 2 * hd), BF16),
            pltpu.VMEM((n // 2, rows, 2 * hd), BF16),
            pltpu.VMEM((n // 2, rows, 2 * hd), BF16),
            pltpu.VMEM((n, 2, hd), F32),
            pltpu.VMEM((groups, 2, hd), F32),
            pltpu.VMEM((lanes, hd), BF16),
            pltpu.VMEM((lanes, hd), BF16),
            dma((n,)), dma((n,)),
            dma((n // 2,)), dma((n // 2,)), dma((n // 2,)), dma((n // 2,)),
            dma((n,)), dma((n,)), dma((groups,)), dma((groups,)),
        ],
        compiler_params=pltpu.CompilerParams(
            collective_id=0, has_side_effects=True,
            vmem_limit_bytes=60 * 2**20),
    )(
        block_order, seq_len, q_raw[0], k_raw[0], values[0], out_grad[0],
        q_gain[None], k_gain[None],
    )
    out = pl.pallas_call(
        store_kernel,
        out_shape=[jax.ShapeDtypeStruct(o.shape, o.dtype) for o in out],
        in_specs=[hbm] * len(out),
        out_specs=[hbm] * len(out),
        scratch_shapes=[pltpu.VMEM(o.shape, o.dtype) for o in out] + [dma((len(out),)), dma((len(out),))],
        compiler_params=pltpu.CompilerParams(vmem_limit_bytes=60 * 2**20),
    )(*out)
    attended, q_grad, k_grad, v_grad, q_gain_grad, k_gain_grad = out
    return (attended[None], q_grad[None], k_grad[None], v_grad[None], q_gain_grad[0], k_gain_grad[0])


def solution(mesh):
    tokens = P("dp", "blk", None)
    in_specs = (tokens, tokens, tokens, tokens, P(), P(), P(), P("dp"))
    out_specs = (tokens, tokens, tokens, tokens, P(), P())
    return jax.shard_map(
        functools.partial(per_device, mesh.shape["blk"], mesh.shape["dp"]),
        mesh=mesh, in_specs=in_specs, out_specs=out_specs, check_vma=False)
```
